512 devices in a mesh: lhs: 16 (over x_hi, y, core), rhs: 32 (over z, x_lo).
Axes of the slice: x: 4 (x_hi: 2, x_lo: 2; x = x_hi * 2 + x_lo), y: 4, z: 16, core: 2. Of those that a mesh axis runs over, the one named last changes fastest.
Arguments:
- head: float32 [16, 32, 512, 256], P('lhs', 'rhs'), may hold values from -2.5 to 2.5
- head_state: float32 [16, 32, 512], P('lhs', 'rhs'), may hold values from 0.001 to 0.01
- tail: float32 [16, 32, 512, 256], P('lhs', 'rhs'), may hold values from -2.5 to 2.5
- tail_state: float32 [16, 32, 512], P('lhs', 'rhs'), may hold values from 0.001 to 0.01
- relations: float32 [1300, 256], replicated, may hold values from -2.5 to 2.5
- relation_state: float32 [1300], replicated, may hold values from 0.5 to 5
- edge_heads: int32 [16, 32, 3, 512], P('lhs', 'rhs'), may hold values from 0 to 511
- edge_rels: int32 [16, 32, 3, 512], P('lhs', 'rhs'), may hold values from 0 to 1299
- edge_tails: int32 [16, 32, 3, 512], P('lhs', 'rhs'), may hold values from 0 to 511
- negatives: int32 [16, 32, 3, 4, 256], P('lhs', 'rhs'), may hold values from 0 to 511
Outputs:
- head_out: float32 [16, 32, 512, 256], P('lhs', 'rhs')
- head_state_out: float32 [16, 32, 512], P('lhs', 'rhs')
- tail_out: float32 [16, 32, 512, 256], P('lhs', 'rhs')
- tail_state_out: float32 [16, 32, 512], P('lhs', 'rhs')
- relations_out: float32 [1300, 256], replicated
- relation_state_out: float32 [1300], replicated
The draws below stay inside these ranges and needn't reach their ends.
All inputs are finite; a program needn't handle non-finite values.
Results may differ from the reference program's by a relative error of at most 0.0003.
Values sent between devices are 32-bit elements; how exact they have to be, the bound alone decides.
A program may use at most 64 MiB of HBM per device.

```python
import math
import jax
import jax.numpy as jnp
from jax import lax

W = 256
RELS = 1300
ROWS = 512
EDGES = 512
BLOCK = 128
NEG = 256
STEPS = 3
BLOCKS = 4
N_LHS = 16
N_RHS = 32


def with_ends(array, stream_key, low, high):
    longest = array.shape.index(max(array.shape))
    spots = []
    for shift in (0, 1):
        where = [jax.random.randint(jax.random.fold_in(stream_key, axis), (), 0, length) for axis, length in enumerate(array.shape)]
        where[longest] = (where[longest] + shift) % array.shape[longest]
        spots.append(tuple(where))
    return array.at[spots[0]].set(low).at[spots[1]].set(high)


def block_scale(key, dims, shards, smallest, high):
    factor_of, own = 1.0, jax.random.fold_in(key, 6)
    for axis_at, parts in shards:
        heights = jnp.exp(jax.random.uniform(jax.random.fold_in(own, axis_at), (parts,), jnp.float32, smallest / len(shards), high / len(shards)))
        factor_of = factor_of * jnp.repeat(heights, dims[axis_at] // parts).reshape([-1 if axis == axis_at else 1 for axis in range(len(dims))])
    return factor_of


def noise(own_key, dims, deviation, bound, pieces=(), kind=jnp.bfloat16):
    gain = block_scale(own_key, dims, pieces, -0.22, 0.18) if pieces else 1.0
    entries = jax.random.normal(own_key, dims, jnp.float32) * deviation * gain
    return jnp.minimum(jnp.maximum(entries, -bound), bound).astype(kind)


def setup_inputs(seed: int = 0) -> dict:
    splits = jax.random.split(jax.random.key(seed), 11)
    return {
        "head": noise(splits[0], (N_LHS, N_RHS, ROWS, W), 0.4, 2.5, ((0, 16), (1, 32)), jnp.float32),
        "head_state": jnp.clip(jnp.exp(math.log(0.01) - 2.30258502 * jax.random.uniform(splits[1], (N_LHS, N_RHS, ROWS), jnp.float32) ** block_scale(splits[1], (N_LHS, N_RHS, ROWS), ((0, 16), (1, 32)), -0.2, 0.2)), 0.001, 0.01),
        "tail": noise(splits[2], (N_LHS, N_RHS, ROWS, W), 0.4, 2.5, ((0, 16), (1, 32)), jnp.float32),
        "tail_state": jnp.clip(jnp.exp(math.log(0.01) - 2.30258502 * jax.random.uniform(splits[3], (N_LHS, N_RHS, ROWS), jnp.float32) ** block_scale(splits[3], (N_LHS, N_RHS, ROWS), ((0, 16), (1, 32)), -0.2, 0.2)), 0.001, 0.01),
        "relations": noise(splits[4], (RELS, W), 0.4, 2.5, (), jnp.float32),
        "relation_state": jnp.clip(jnp.exp(jax.random.uniform(splits[5], (RELS,), jnp.float32, math.log(0.5), math.log(5.0))), 0.5, 5.0),
        "edge_heads": with_ends(jax.random.randint(splits[6], (N_LHS, N_RHS, STEPS, EDGES), 0, ROWS), jax.random.fold_in(splits[6], 1), 0, ROWS - 1).astype(jnp.int32),
        "edge_rels": with_ends(jax.random.randint(splits[7], (N_LHS, N_RHS, STEPS, EDGES), 0, RELS), jax.random.fold_in(splits[7], 1), 0, RELS - 1).astype(jnp.int32),
        "edge_tails": with_ends(jax.random.randint(splits[8], (N_LHS, N_RHS, STEPS, EDGES), 0, ROWS), jax.random.fold_in(splits[8], 1), 0, ROWS - 1).astype(jnp.int32),
        "negatives": with_ends(jax.random.randint(splits[9], (N_LHS, N_RHS, STEPS, BLOCKS, NEG), 0, ROWS), jax.random.fold_in(splits[9], 1), 0, ROWS - 1).astype(jnp.int32),
    }


learn_rate = 0.1

def adagrad(param, state, grad):
    state_new = state + lax.optimization_barrier(jnp.mean(grad * grad, axis=-1))
    return (param - learn_rate * grad * lax.rsqrt(state_new)[..., None], state_new)

def block_terms(pair):
    q_block, n_block = pair
    scores = jnp.dot(q_block, n_block.T, preferred_element_type=jnp.float32)
    dneg = (jax.nn.sigmoid(scores) / NEG).astype(jnp.bfloat16)
    gq_neg = jnp.dot(dneg, n_block, preferred_element_type=jnp.float32)
    g_neg = jnp.dot(dneg.T, q_block, preferred_element_type=jnp.float32)
    return (gq_neg, g_neg)

def bucket(head, tail, rel, heads_idx, rels_idx, tails_idx, negs):
    half = W // 2
    h_rows = head[heads_idx]
    r_rows = rel[rels_idx]
    t_rows = tail[tails_idx]
    h_re, h_im = (h_rows[:, :half], h_rows[:, half:])
    r_re, r_im = (r_rows[:, :half], r_rows[:, half:])
    q_rows = jnp.concatenate([h_re * r_re - h_im * r_im, h_re * r_im + h_im * r_re], axis=1)
    pos = lax.optimization_barrier(jnp.sum(q_rows * t_rows, axis=1))
    dpos = -jax.nn.sigmoid(-pos)
    q_half = q_rows.astype(jnp.bfloat16).reshape(BLOCKS, BLOCK, W)
    n_half = tail[negs].astype(jnp.bfloat16)
    gq_neg, g_neg = lax.map(block_terms, (q_half, n_half))
    grad_q = dpos[:, None] * t_rows + gq_neg.reshape(EDGES, W)
    gq_re, gq_im = (grad_q[:, :half], grad_q[:, half:])
    grad_h = jnp.concatenate([gq_re * r_re + gq_im * r_im, gq_im * r_re - gq_re * r_im], axis=1)
    grad_r = jnp.concatenate([gq_re * h_re + gq_im * h_im, gq_im * h_re - gq_re * h_im], axis=1)
    grad_head = jnp.zeros((ROWS, W), jnp.float32).at[heads_idx].add(grad_h)
    grad_tail = jnp.zeros((ROWS, W), jnp.float32).at[tails_idx].add(dpos[:, None] * q_rows)
    grad_tail = grad_tail.at[negs.reshape(-1)].add(g_neg.reshape(BLOCKS * NEG, W))
    grad_rel = jnp.zeros((RELS, W), jnp.float32).at[rels_idx].add(grad_r)
    return (grad_head, grad_tail, grad_rel)

def reference(head, head_state, tail, tail_state, relations, relation_state, edge_heads, edge_rels, edge_tails, negatives):
    count = N_LHS * N_RHS
    heads_now = head.reshape(count, ROWS, W)
    heads_sum = head_state.reshape(count, ROWS)
    tails_now = tail.reshape(count, ROWS, W)
    tails_sum = tail_state.reshape(count, ROWS)
    flat_h = edge_heads.reshape(count, STEPS, EDGES)
    flat_r = edge_rels.reshape(count, STEPS, EDGES)
    flat_t = edge_tails.reshape(count, STEPS, EDGES)
    flat_n = negatives.reshape(count, STEPS, BLOCKS, NEG)
    for step in range(STEPS):
        rel_now = relations

        def visit(total, item):
            h_slab, h_sum, t_slab, t_sum, e_h, e_r, e_t, e_n = item
            g_head, g_tail, g_rel = bucket(h_slab, t_slab, rel_now, e_h, e_r, e_t, e_n)
            h_new, hs_new = adagrad(h_slab, h_sum, g_head)
            t_new, ts_new = adagrad(t_slab, t_sum, g_tail)
            return (total + g_rel, (h_new, hs_new, t_new, ts_new))
        total, (heads_now, heads_sum, tails_now, tails_sum) = lax.scan(visit, jnp.zeros((RELS, W), jnp.float32), (heads_now, heads_sum, tails_now, tails_sum, flat_h[:, step], flat_r[:, step], flat_t[:, step], flat_n[:, step]))
        relations, relation_state = adagrad(relations, relation_state, total)
        if step + 1 < STEPS:
            heads_now = jnp.roll(heads_now.reshape(N_LHS, N_RHS, ROWS, W), 1, axis=0).reshape(count, ROWS, W)
            heads_sum = jnp.roll(heads_sum.reshape(N_LHS, N_RHS, ROWS), 1, axis=0).reshape(count, ROWS)
            tails_now = jnp.roll(tails_now.reshape(N_LHS, N_RHS, ROWS, W), 1, axis=1).reshape(count, ROWS, W)
            tails_sum = jnp.roll(tails_sum.reshape(N_LHS, N_RHS, ROWS), 1, axis=1).reshape(count, ROWS)
    return (heads_now.reshape(N_LHS, N_RHS, ROWS, W), heads_sum.reshape(N_LHS, N_RHS, ROWS), tails_now.reshape(N_LHS, N_RHS, ROWS, W), tails_sum.reshape(N_LHS, N_RHS, ROWS), relations, relation_state)
```

```python
import functools

import jax
import jax.numpy as jnp
from jax import lax
from jax.experimental import pallas as pl
from jax.experimental.pallas import tpu as pltpu
from jax.sharding import PartitionSpec as P

LEARN_RATE = 0.1
MESH = pl.DeviceIdType.MESH
F32, BF16 = jnp.float32, jnp.bfloat16

NX, NY, NZ = 4, 4, 16
XY = NX * NY
W, HALF, ROWS, EDGES, RELS, STEPS = 256, 128, 512, 512, 1300, 3
BLOCKS, NEG = 4, 256
BLOCK = EDGES // BLOCKS
TILES = -(-RELS // 128)
RPAD = TILES * 128
SLAB = W + 8

OFFS = sorted(
    [(dx, dy) for dx in range(NX) for dy in range(NY) if (dx, dy) != (0, 0)],
    key=lambda o: -(min(o[0], NX - o[0]) + min(o[1], NY - o[1])),
)
N_OFF = len(OFFS)
OWN = [j * NZ // TILES for j in range(TILES)]


def coords():
    a, b = lax.axis_index("lhs"), lax.axis_index("rhs")
    core, y, xh = lax.rem(a, 2), lax.rem(lax.div(a, 2), NY), lax.div(a, 2 * NY)
    return xh * 2 + lax.rem(b, 2), y, lax.div(b, 2), core


def device(x, y, z, core):
    return ((lax.div(x, 2) * NY + y) * 2 + core, z * 2 + lax.rem(x, 2))


def nn(a, b):
    return jnp.dot(a, b, preferred_element_type=F32)


def nt(a, b):
    return lax.dot_general(a, b, (((1,), (1,)), ((), ())), preferred_element_type=F32)


def split(x):
    hi = x.astype(BF16)
    return hi, (x - hi.astype(F32)).astype(BF16)


def one_hot(index, count):
    place = lax.broadcasted_iota(jnp.int32, (count, index.shape[1]), 0)
    return jnp.where(place == index, 1.0, 0.0).astype(BF16)


def kernel(
    head, head_sum, tail, tail_sum, rel, rel_sum, eh, er, et, ng,
    head_out, head_sum_out, tail_out, tail_sum_out, rel_out, rel_sum_out,
    heads, tails, relT, rsum, relhl, oh_r, oh_h, oh_t, cnt,
    hT, tT, rT, tb, tbT, q, dpos, qb, phi, plo, gq, grhl,
    g, total, crecv, acc, xrecv, zrecv, mine,
    s_c, r_c, s_x, r_x, s_z, r_z, s_zg, r_zg, s_xg, r_xg, s_cg, r_cg, s_h, r_h, s_t, r_t,
):
    x, y, z, core = coords()
    me = x * NY + y
    lo, other = core * XY, (1 - core) * XY
    a, b = lax.axis_index("lhs"), lax.axis_index("rhs")
    partner = device(x, y, z, 1 - core)
    head_to = (lax.rem(a + 1, 2 * NX // 2 * NY), b)
    head_from = (lax.rem(a + 2 * NX // 2 * NY - 1, 2 * NX // 2 * NY), b)
    tail_to = (a, lax.rem(b + 1, 2 * NZ))
    tail_from = (a, lax.rem(b + 2 * NZ - 1, 2 * NZ))
    order = []
    for dx, dy in OFFS + [(0, 0)]:
        tx, ty = lax.rem(x + dx, NX), lax.rem(y + dy, NY)
        order.append((device(tx, ty, z, core), tx * NY + ty))

    barrier = pltpu.get_barrier_semaphore()
    peers = [partner, head_to, head_from, tail_to, tail_from]
    peers += [d for d, _ in order[:-1]]
    peers += [device(x, y, lax.rem(z + dz, NZ), core) for dz in range(1, NZ)]
    for d in peers:
        pl.semaphore_signal(barrier, inc=1, device_id=d, device_id_type=MESH)

    def prep_index(s):
        oh_r[...] = one_hot(er[s], RPAD)
        oh_h[...] = one_hot(eh[s], ROWS)
        oh_t[...] = one_hot(et[s], ROWS)
        ones = jnp.ones((NEG, BLOCK), BF16)
        for k in range(BLOCKS):
            cnt[:, k * BLOCK:(k + 1) * BLOCK] = nn(one_hot(ng[s, k], ROWS), ones)

    def gather(wide, hot):
        both = nn(jnp.concatenate(split(wide), axis=0), hot)
        return both[:W] + both[W:]

    def prep_slab(s):
        hT[...] = gather(heads[s, :W], oh_h[...])
        slab = tails[s, :W]
        tT[...] = gather(slab, oh_t[...])
        tbT[...] = slab.astype(BF16)
        tb[...] = slab.T.astype(BF16)

    def update(slab, total_grad):
        new = slab[W:W + 1] + jnp.mean(total_grad * total_grad, axis=0, keepdims=True)
        slab[W:W + 1] = new
        slab[:W] = slab[:W] - LEARN_RATE * total_grad * lax.rsqrt(new)

    heads[0, :W] = head[...].T
    heads[0, W:W + 1] = head_sum[...]
    tails[0, :W] = tail[...].T
    tails[0, W:W + 1] = tail_sum[...]
    rsum[...] = jnp.ones_like(rsum)
    rsum[:, :RELS] = rel_sum[...]
    for j in range(TILES):
        lanes = slice(j * 128, (j + 1) * 128)
        count = min(128, RELS - j * 128)
        part = rel[j * 128:j * 128 + count]
        if count < 128:
            part = jnp.concatenate([part, jnp.zeros((128 - count, W), F32)], axis=0)
        part = part.T
        relT[:, lanes] = part
        relhl[:W, lanes], relhl[W:, lanes] = split(part)
    prep_index(0)
    prep_slab(0)
    pl.semaphore_wait(barrier, len(peers))

    def move(slabs, s, send, recv, to):
        return pltpu.make_async_remote_copy(
            src_ref=slabs.at[s], dst_ref=slabs.at[s + 1], send_sem=send, recv_sem=recv,
            device_id=to, device_id_type=MESH,
        )

    def step(s, carry):
        both = nn(relhl[...], oh_r[...])
        r_all = both[:W] + both[W:]
        rT[...] = r_all
        r_re, r_im = r_all[:HALF], r_all[HALF:]
        h_re, h_im = hT[:HALF], hT[HALF:]
        q_re, q_im = h_re * r_re - h_im * r_im, h_re * r_im + h_im * r_re
        q[:HALF], q[HALF:] = q_re, q_im
        pos = jnp.sum(q_re * tT[:HALF] + q_im * tT[HALF:], axis=0, keepdims=True)
        dp = -jax.nn.sigmoid(-pos)
        dpos[...] = dp
        qb[:HALF], qb[HALF:] = q_re.astype(BF16), q_im.astype(BF16)
        scores = nn(tb[...], qb[...])
        dneg = (jax.nn.sigmoid(scores) * (1.0 / NEG)).astype(BF16)
        phi[...], plo[...] = split(dneg.astype(F32) * cnt[...])
        grad_q = dp * tT[...] + (nn(tbT[...], phi[...]) + nn(tbT[...], plo[...]))
        gq[...] = grad_q
        g_re, g_im = grad_q[:HALF], grad_q[HALF:]
        for k, term in enumerate((g_re * h_re + g_im * h_im, g_im * h_re - g_re * h_im)):
            grhl[k, :HALF], grhl[k, HALF:] = split(term)

        def relation_grad(k):
            for j in range(TILES):
                lanes = slice(j * 128, (j + 1) * 128)
                both = nt(grhl[k], oh_r[lanes])
                g[pl.ds(k * XY, XY), :, lanes] = (both[:HALF] + both[HALF:]).reshape(XY, 8, 128)

        relation_grad(1 - core)
        cores = []
        for k, (_, t) in enumerate(order):
            c = pltpu.make_async_remote_copy(
                src_ref=g.at[other + t], dst_ref=crecv.at[s, t], send_sem=s_c.at[k], recv_sem=r_c.at[s, k],
                device_id=partner, device_id_type=MESH,
            )
            c.start()
            cores.append(c)
        relation_grad(core)
        planes = []
        for k, (d, t) in enumerate(order):
            cores[k].wait_recv()
            acc[t] = g[lo + t] + crecv[s, t]
            if k < N_OFF:
                c = pltpu.make_async_remote_copy(
                    src_ref=acc.at[t], dst_ref=xrecv.at[s, k], send_sem=s_x.at[k], recv_sem=r_x.at[s, k],
                    device_id=d, device_id_type=MESH,
                )
                c.start()
                planes.append(c)

        g_re, g_im = gq[:HALF], gq[HALF:]
        r_re, r_im = rT[:HALF], rT[HALF:]
        term = jnp.concatenate([g_re * r_re + g_im * r_im, g_im * r_re - g_re * r_im], axis=0)
        both = nt(jnp.concatenate(split(term), axis=0), oh_h[...])
        update(heads.at[s], both[:W] + both[W:])
        term = dpos[...] * q[...]
        both = nt(jnp.concatenate(split(term), axis=0), oh_t[...])
        neg = nt(qb[...], phi[...]) + nt(qb[...], plo[...])
        update(tails.at[s], both[:W] + both[W:] + neg)

        part = acc[me]
        for k in range(N_OFF):
            planes[k].wait_recv()
            part = part + xrecv[s, k]
        mine[...] = part

        def to_owner(j, slot):
            return pltpu.make_async_remote_copy(
                src_ref=mine.at[:, pl.ds(j * 128, 128)], dst_ref=zrecv.at[s, slot], send_sem=s_z.at[j],
                recv_sem=r_z.at[s], device_id=device(x, y, OWN[j], core), device_id_type=MESH,
            )

        def to_all(j, zt, k):
            ref = total.at[s, lo + me, :, pl.ds(j * 128, 128)]
            return pltpu.make_async_remote_copy(
                src_ref=ref, dst_ref=ref, send_sem=s_zg.at[k], recv_sem=r_zg.at[s, j],
                device_id=device(x, y, zt, core), device_id_type=MESH,
            )

        for j in range(TILES):
            @pl.when(z != OWN[j])
            def _():
                to_owner(j, lax.rem(z - OWN[j] + NZ, NZ) - 1).start()

        @pl.when(s < STEPS - 1)
        def _():
            move(heads, s, s_h, r_h.at[s], head_to).start()
            move(tails, s, s_t, r_t.at[s], tail_to).start()

        for j in range(TILES):
            @pl.when(z == OWN[j])
            def _():
                pltpu.make_async_copy(zrecv.at[s], zrecv.at[s], r_z.at[s]).wait()
                tile = mine[:, j * 128:(j + 1) * 128]
                for k in range(NZ - 1):
                    tile = tile + zrecv[s, k]
                total[s, lo + me, :, j * 128:(j + 1) * 128] = tile
                for k in sorted(range(1, NZ), key=lambda d: -min(d, NZ - d)):
                    to_all(j, lax.rem(z + k, NZ), k - 1).start()

        for j in range(TILES):
            @pl.when(z != OWN[j])
            def _():
                to_all(j, z, 0).wait_recv()

        def to_core(t, k):
            ref = total.at[s, lo + t]
            return pltpu.make_async_remote_copy(
                src_ref=ref, dst_ref=ref, send_sem=s_cg.at[k], recv_sem=r_cg.at[s, k],
                device_id=partner, device_id_type=MESH,
            )

        spread = []
        for k, (d, t) in enumerate(order[:-1]):
            ref = total.at[s, lo + me]
            c = pltpu.make_async_remote_copy(
                src_ref=ref, dst_ref=ref, send_sem=s_xg.at[k], recv_sem=r_xg.at[s, k],
                device_id=d, device_id_type=MESH,
            )
            c.start()
            spread.append(c)
        passed = [to_core(me, N_OFF)]
        passed[0].start()

        @pl.when(s < STEPS - 1)
        def _():
            prep_index(s + 1)
            for c in (move(heads, s, s_h, r_h.at[s], head_to), move(tails, s, s_t, r_t.at[s], tail_to)):
                c.wait_recv()
                c.wait_send()
            prep_slab(s + 1)

        @pl.when(s == STEPS - 1)
        def _():
            head_out[...] = heads[STEPS - 1, :W].T
            head_sum_out[...] = heads[STEPS - 1, W:W + 1]
            tail_out[...] = tails[STEPS - 1, :W].T
            tail_sum_out[...] = tails[STEPS - 1, W:W + 1]

        for k, (dx, dy) in reversed(list(enumerate(OFFS))):
            spread[k].wait_recv()
            c = to_core(lax.rem(x - dx + NX, NX) * NY + lax.rem(y - dy + NY, NY), k)
            c.start()
            passed.append(c)
        for c in passed:
            c.wait_recv()

        for j in range(TILES):
            lanes = slice(j * 128, (j + 1) * 128)
            grad = total[s, :, :, lanes].reshape(W, 128)
            new = rsum[:, lanes] + jnp.mean(grad * grad, axis=0, keepdims=True)
            rsum[:, lanes] = new
            part = relT[:, lanes] - LEARN_RATE * grad * lax.rsqrt(new)
            relT[:, lanes] = part
            relhl[:W, lanes], relhl[W:, lanes] = split(part)

        for c in cores + planes + spread + passed:
            c.wait_send()
        for j in range(TILES):
            @pl.when(z != OWN[j])
            def _():
                to_owner(j, 0).wait_send()

            @pl.when(z == OWN[j])
            def _():
                for k in range(NZ - 1):
                    to_all(j, z, k).wait_send()
        return carry

    lax.fori_loop(0, STEPS, step, 0)

    rel_sum_out[...] = rsum[:, :RELS]
    for j in range(TILES):
        count = min(128, RELS - j * 128)
        rel_out[j * 128:j * 128 + count] = relT[:, j * 128:(j + 1) * 128].T[:count]


def body(head, head_state, tail, tail_state, relations, relation_state, edge_heads, edge_rels, edge_tails, negatives):
    dma, vmem = pltpu.SemaphoreType.DMA, pltpu.VMEM
    out = pl.pallas_call(
        kernel,
        out_shape=(
            jax.ShapeDtypeStruct((ROWS, W), F32),
            jax.ShapeDtypeStruct((1, ROWS), F32),
            jax.ShapeDtypeStruct((ROWS, W), F32),
            jax.ShapeDtypeStruct((1, ROWS), F32),
            jax.ShapeDtypeStruct((RELS, W), F32),
            jax.ShapeDtypeStruct((1, RELS), F32),
        ),
        in_specs=[pl.BlockSpec(memory_space=pltpu.VMEM)] * 10,
        out_specs=[pl.BlockSpec(memory_space=pltpu.VMEM)] * 6,
        scratch_shapes=[
            vmem((STEPS, SLAB, ROWS), F32),
            vmem((STEPS, SLAB, ROWS), F32),
            vmem((W, RPAD), F32),
            vmem((1, RPAD), F32),
            vmem((2 * W, RPAD), BF16),
            vmem((RPAD, EDGES), BF16),
            vmem((ROWS, EDGES), BF16),
            vmem((ROWS, EDGES), BF16),
            vmem((ROWS, EDGES), F32),
            vmem((W, EDGES), F32),
            vmem((W, EDGES), F32),
            vmem((W, EDGES), F32),
            vmem((ROWS, W), BF16),
            vmem((W, ROWS), BF16),
            vmem((W, EDGES), F32),
            vmem((1, EDGES), F32),
            vmem((W, EDGES), BF16),
            vmem((ROWS, EDGES), BF16),
            vmem((ROWS, EDGES), BF16),
            vmem((W, EDGES), F32),
            vmem((2, W, EDGES), BF16),
            vmem((2 * XY, 8, RPAD), F32),
            vmem((STEPS, 2 * XY, 8, RPAD), F32),
            vmem((STEPS, XY, 8, RPAD), F32),
            vmem((XY, 8, RPAD), F32),
            vmem((STEPS, N_OFF, 8, RPAD), F32),
            vmem((STEPS, NZ - 1, 8, 128), F32),
            vmem((8, RPAD), F32),
            dma((XY,)), dma((STEPS, XY)),
            dma((N_OFF,)), dma((STEPS, N_OFF)),
            dma((TILES,)), dma((STEPS,)),
            dma((NZ - 1,)), dma((STEPS, TILES)),
            dma((N_OFF,)), dma((STEPS, N_OFF)),
            dma((XY,)), dma((STEPS, XY)),
            dma, dma((STEPS,)),
            dma, dma((STEPS,)),
        ],
        compiler_params=pltpu.CompilerParams(
            collective_id=0, has_side_effects=True, vmem_limit_bytes=48 * 2**20
        ),
        name="window",
    )(
        head.reshape(ROWS, W),
        head_state.reshape(1, ROWS),
        tail.reshape(ROWS, W),
        tail_state.reshape(1, ROWS),
        relations,
        relation_state.reshape(1, RELS),
        edge_heads.reshape(STEPS, 1, EDGES),
        edge_rels.reshape(STEPS, 1, EDGES),
        edge_tails.reshape(STEPS, 1, EDGES),
        negatives.reshape(STEPS, BLOCKS, 1, NEG),
    )
    return (
        out[0].reshape(1, 1, ROWS, W),
        out[1].reshape(1, 1, ROWS),
        out[2].reshape(1, 1, ROWS, W),
        out[3].reshape(1, 1, ROWS),
        out[4],
        out[5].reshape(RELS),
    )


def solution(mesh):
    slab, sums = P("lhs", "rhs", None, None), P("lhs", "rhs", None)
    return jax.shard_map(
        body,
        mesh=mesh,
        in_specs=(slab, sums, slab, sums, P(), P(), slab, slab, slab, P("lhs", "rhs", None, None, None)),
        out_specs=(slab, sums, slab, sums, P(), P()),
        check_vma=False,
    )
```

```python
import functools

import jax
import jax.numpy as jnp
from jax import lax
from jax.experimental import pallas as pl
from jax.experimental.pallas import tpu as pltpu
from jax.sharding import PartitionSpec as P

LEARN_RATE = 0.1
MESH = pl.DeviceIdType.MESH
F32, BF16 = jnp.float32, jnp.bfloat16

NX, NY, NZ = 4, 4, 16
N_LHS, N_RHS = 2 * NY * 2, NZ * 2
XY = NX * NY
W, HALF, ROWS, EDGES, RELS, STEPS = 256, 128, 512, 512, 1300, 3
BLOCKS, NEG = 4, 256
BLOCK = EDGES // BLOCKS
TILES = -(-RELS // 128)
RPAD = TILES * 128
SLAB = W + 8

PARTS = ((0, 6), (6, 11))
N_PARTS = len(PARTS)
OFFS = sorted(
    [(dx, dy) for dx in range(NX) for dy in range(NY) if (dx, dy) != (0, 0)],
    key=lambda o: (min(o[0], NX - o[0]) + min(o[1], NY - o[1])),
)
N_OFF = len(OFFS)
OWN = [j * NZ // TILES for j in range(TILES)]
COMPUTE = True
MOVE = True
VMEM_LIMIT = 60 * 2**20


def coords():
    a, b = lax.axis_index("lhs"), lax.axis_index("rhs")
    core, y, xh = lax.rem(a, 2), lax.rem(lax.div(a, 2), NY), lax.div(a, 2 * NY)
    return xh * 2 + lax.rem(b, 2), y, lax.div(b, 2), core


def device(x, y, z, core):
    return ((lax.div(x, 2) * NY + y) * 2 + core, z * 2 + lax.rem(x, 2))


def nn(a, b):
    return jnp.dot(a, b, preferred_element_type=F32)


def nt(a, b):
    return lax.dot_general(a, b, (((1,), (1,)), ((), ())), preferred_element_type=F32)


def split(x):
    hi = x.astype(BF16)
    return hi, (x - hi.astype(F32)).astype(BF16)


def one_hot(index, count):
    place = lax.broadcasted_iota(jnp.int32, (count, index.shape[1]), 0)
    return jnp.where(place == index, 1.0, 0.0).astype(BF16)


def remote(src, dst, send, recv, to):
    return pltpu.make_async_remote_copy(
        src_ref=src, dst_ref=dst, send_sem=send, recv_sem=recv, device_id=to, device_id_type=MESH
    )


def wait_bytes(like, sem):
    pltpu.make_async_copy(like, like, sem).wait()


def kernel(
    head_in, head_sum_in, tail_in, tail_sum_in, rel_in, rel_sum_in, eh_in, er_in, et_in, ng_in,
    head_out, head_sum_out, tail_out, tail_sum_out, rel_out, rel_sum_out,
    head, tail, rel, eh, er, et, ng, head_sum, tail_sum, rel_sum, s_in,
    heads, tails, relT, rsum, relhl, oh_r, oh_h, oh_t, cnt,
    hT, tT, rT, tb, tbT, q, dpos, qb, phi, plo, gq, grhl,
    g, total, crecv, acc, xrecv, zrecv, mine,
    s_c, r_c, s_x, r_x, s_z, r_z, s_zg, r_zg, s_xg, r_xg, s_cg, r_cg, s_h, r_h, s_t, r_t, s_tz, r_tz,
):
    x, y, z, core = coords()
    me = x * NY + y
    lo, other = core * XY, (1 - core) * XY
    a, b = lax.axis_index("lhs"), lax.axis_index("rhs")
    partner = device(x, y, z, 1 - core)
    head_to, head_from = (lax.rem(a + 1, N_LHS), b), (lax.rem(a + N_LHS - 1, N_LHS), b)
    plane = []
    for dx, dy in OFFS:
        tx, ty = lax.rem(x + dx, NX), lax.rem(y + dy, NY)
        plane.append((device(tx, ty, z, core), tx * NY + ty))

    barrier = pltpu.get_barrier_semaphore()
    peers = [device(x, y, lax.rem(z + dz, NZ), core) for dz in range(1, NZ)]
    peers += [d for d, _ in plane] + [partner, head_to, head_from]
    for d in peers:
        pl.semaphore_signal(barrier, inc=1, device_id=d, device_id_type=MESH)

    loads = [
        (er_in, er), (eh_in, eh), (et_in, et), (ng_in, ng), (head_in, head), (tail_in, tail), (rel_in, rel),
        (head_sum_in, head_sum), (tail_sum_in, tail_sum), (rel_sum_in, rel_sum),
    ]
    loads = [pltpu.make_async_copy(src, dst, s_in.at[k]) for k, (src, dst) in enumerate(loads)]
    for c in loads:
        c.start()

    stores = [
        (head, head_out), (head_sum, head_sum_out), (tail, tail_out), (tail_sum, tail_sum_out),
        (rel_sum, rel_sum_out),
    ]
    for first, last in PARTS:
        rows = pl.ds(first * 128, min(last * 128, RELS) - first * 128)
        stores.append((rel.at[rows], rel_out.at[rows]))
    stores = [pltpu.make_async_copy(src, dst, s_in.at[k]) for k, (src, dst) in enumerate(stores)]

    def prep_index(s):
        oh_r[...] = one_hot(er[s], RPAD)
        oh_h[...] = one_hot(eh[s], ROWS)
        oh_t[...] = one_hot(et[s], ROWS)
        ones = jnp.ones((NEG, BLOCK), BF16)
        for k in range(BLOCKS):
            cnt[:, k * BLOCK:(k + 1) * BLOCK] = nn(one_hot(ng[s, k:k + 1], ROWS), ones)

    def gather(wide, hot):
        both = nn(jnp.concatenate(split(wide), axis=0), hot)
        return both[:W] + both[W:]

    def prep_head(s):
        hT[...] = gather(heads[s, :W], oh_h[...])

    def prep_tail(s):
        slab = tails[s, :W]
        tT[...] = gather(slab, oh_t[...])
        tbT[...] = slab.astype(BF16)
        tb[...] = slab.T.astype(BF16)

    def update(slab, total_grad):
        new = slab[W:W + 1] + jnp.mean(total_grad * total_grad, axis=0, keepdims=True)
        slab[W:W + 1] = new
        slab[:W] = slab[:W] - LEARN_RATE * total_grad * lax.rsqrt(new)

    def lanes(p):
        return pl.ds(PARTS[p][0] * 128, (PARTS[p][1] - PARTS[p][0]) * 128)

    def relation_grad(k, p):
        both = nt(grhl[k], oh_r[lanes(p)])
        g[pl.ds(k * XY, XY), :, lanes(p)] = (both[:HALF] + both[HALF:]).reshape(XY, 8, -1)

    def gather_relations(p):
        both = nn(relhl[:, lanes(p)], oh_r[lanes(p)])
        part = both[:W] + both[W:]
        rT[...] = part if p == 0 else rT[...] + part

    def terms():
        r_re, r_im = rT[:HALF], rT[HALF:]
        h_re, h_im = hT[:HALF], hT[HALF:]
        q_re, q_im = h_re * r_re - h_im * r_im, h_re * r_im + h_im * r_re
        q[:HALF], q[HALF:] = q_re, q_im
        pos = jnp.sum(q_re * tT[:HALF] + q_im * tT[HALF:], axis=0, keepdims=True)
        dp = -jax.nn.sigmoid(-pos)
        dpos[...] = dp
        qb[:HALF], qb[HALF:] = q_re.astype(BF16), q_im.astype(BF16)
        scores = nn(tb[...], qb[...])
        dneg = (jax.nn.sigmoid(scores) * (1.0 / NEG)).astype(BF16)
        phi[...], plo[...] = split(dneg.astype(F32) * cnt[...])
        grad_q = dp * tT[...] + (nn(tbT[...], phi[...]) + nn(tbT[...], plo[...]))
        gq[...] = grad_q
        g_re, g_im = grad_q[:HALF], grad_q[HALF:]
        for k, term in enumerate((g_re * h_re + g_im * h_im, g_im * h_re - g_re * h_im)):
            grhl[k, :HALF], grhl[k, HALF:] = split(term)
        relation_grad(1 - core, 0)

    def head_update(s):
        g_re, g_im = gq[:HALF], gq[HALF:]
        r_re, r_im = rT[:HALF], rT[HALF:]
        term = jnp.concatenate([g_re * r_re + g_im * r_im, g_im * r_re - g_re * r_im], axis=0)
        both = nt(jnp.concatenate(split(term), axis=0), oh_h[...])
        update(heads.at[s], both[:W] + both[W:])

    def tail_update(s):
        term = dpos[...] * q[...]
        both = nt(jnp.concatenate(split(term), axis=0), oh_t[...])
        neg = nt(qb[...], phi[...]) + nt(qb[...], plo[...])
        update(tails.at[s], both[:W] + both[W:] + neg)

    if COMPUTE:
        for c in loads[:4]:
            c.wait()
        prep_index(0)
        for c in loads[4:]:
            c.wait()
        rsum[...] = jnp.ones_like(rsum)
        rsum[:, :RELS] = rel_sum[...].reshape(1, RELS)
        heads[0, :W] = head[...].T
        heads[0, W:W + 1] = head_sum[...]
        prep_head(0)
        tails[0, :W] = tail[...].T
        tails[0, W:W + 1] = tail_sum[...]
        prep_tail(0)
        for j in range(TILES):
            at = slice(j * 128, (j + 1) * 128)
            count = min(128, RELS - j * 128)
            part = rel[j * 128:j * 128 + count]
            if count < 128:
                part = jnp.concatenate([part, jnp.zeros((128 - count, W), F32)], axis=0)
            part = part.T
            relT[:, at] = part
            relhl[:W, at], relhl[W:, at] = split(part)
        for p in range(N_PARTS):
            gather_relations(p)
        terms()
    else:
        for c in loads:
            c.wait()
    pl.semaphore_wait(barrier, len(peers))

    x_lo = lax.rem(b, 2)
    tile = z - lax.div(z, 3)
    owner = jnp.logical_or(z == 0, lax.rem(z, 3) != 0)

    def step(s, carry):
        more = s < STEPS - 1
        move_head = remote(heads.at[s], heads.at[s + 1], s_h, r_h.at[s], head_to)
        move_z = remote(tails.at[s], tails.at[STEPS + s], s_tz, r_tz.at[s], (a, lax.rem(b + 2, N_RHS)))
        move_x = remote(
            tails.at[s + x_lo * STEPS], tails.at[s + 1], s_t, r_t.at[s], (a, b + 1 - 2 * x_lo)
        )

        def to_other(p):
            return remote(
                g.at[pl.ds(other, XY), :, lanes(p)], crecv.at[s, :, :, lanes(p)], s_c.at[p], r_c.at[s, p], partner
            )

        def to_plane(p):
            to_other(p).wait_recv()
            for k, (d, t) in enumerate(plane):
                acc[t, :, lanes(p)] = g[lo + t, :, lanes(p)] + crecv[s, t, :, lanes(p)]
                remote(acc.at[t, :, lanes(p)], xrecv.at[s, k, :, lanes(p)], s_x.at[p], r_x.at[s, p], d).start()
            mine[:, lanes(p)] = g[lo + me, :, lanes(p)] + crecv[s, me, :, lanes(p)]

        to_other(0).start()
        if COMPUTE:
            relation_grad(1 - core, 1)
        to_other(1).start()
        if COMPUTE:
            relation_grad(core, 0)
        to_plane(0)
        if COMPUTE:
            relation_grad(core, 1)
        to_plane(1)

        if COMPUTE:
            tail_update(s)
        if MOVE:
            @pl.when(jnp.logical_and(more, x_lo == 1))
            def _():
                move_z.start()
        if COMPUTE:
            head_update(s)

        for p in range(N_PARTS):
            wait_bytes(xrecv.at[s, :, :, lanes(p)], r_x.at[s, p])
            part = mine[:, lanes(p)]
            for k in range(N_OFF):
                part = part + xrecv[s, k, :, lanes(p)]
            mine[:, lanes(p)] = part
            for j in range(*PARTS[p]):
                @pl.when(z != OWN[j])
                def _():
                    remote(
                        mine.at[:, pl.ds(j * 128, 128)], zrecv.at[s, lax.rem(z - OWN[j] + NZ, NZ) - 1],
                        s_z, r_z.at[s], device(x, y, OWN[j], core),
                    ).start()

        if MOVE:
            @pl.when(more)
            def _():
                move_head.start()

        @pl.when(owner)
        def _():
            wait_bytes(zrecv.at[s], r_z.at[s])
            at = pl.ds(pl.multiple_of(tile * 128, 128), 128)
            part = mine[:, at]
            for k in range(NZ - 1):
                part = part + zrecv[s, k]
            total[s, lo + me, :, at] = part
            ref = total.at[s, lo + me, :, at]
            which = jnp.where(tile >= PARTS[0][1], 1, 0)
            for k in sorted(range(1, NZ), key=lambda d: -min(d, NZ - d)):
                to = device(x, y, lax.rem(z + k, NZ), core)
                remote(ref, ref, s_zg, r_zg.at[s, which], to).start()

        if MOVE:
            @pl.when(more)
            def _():
                @pl.when(x_lo == 1)
                def _():
                    move_z.wait_recv()

                move_x.start()

        def to_core(p):
            ref = total.at[s, pl.ds(lo, XY), :, lanes(p)]
            return remote(ref, ref, s_cg.at[p], r_cg.at[s, p], partner)

        for p in range(N_PARTS):
            first, last = PARTS[p]
            mine_too = jnp.logical_and(owner, jnp.logical_and(tile >= first, tile < last))

            @pl.when(mine_too)
            def _():
                wait_bytes(mine.at[:, pl.ds(0, (last - first - 1) * 128)], r_zg.at[s, p])

            @pl.when(jnp.logical_not(mine_too))
            def _():
                wait_bytes(mine.at[:, pl.ds(0, (last - first) * 128)], r_zg.at[s, p])

            ref = total.at[s, lo + me, :, lanes(p)]
            for d, _ in plane:
                remote(ref, ref, s_xg.at[p], r_xg.at[s, p], d).start()

        if COMPUTE:
            @pl.when(more)
            def _():
                prep_index(s + 1)

        wait_bytes(xrecv.at[s, :, :, lanes(0)], r_xg.at[s, 0])
        to_core(0).start()

        @pl.when(more)
        def _():
            if MOVE:
                move_head.wait()
            if COMPUTE:
                prep_head(s + 1)

        wait_bytes(xrecv.at[s, :, :, lanes(1)], r_xg.at[s, 1])
        to_core(1).start()

        @pl.when(more)
        def _():
            if MOVE:
                move_x.wait()

                @pl.when(x_lo == 1)
                def _():
                    move_z.wait_send()
            if COMPUTE:
                prep_tail(s + 1)

        if COMPUTE:
            @pl.when(jnp.logical_not(more))
            def _():
                head[...] = heads[STEPS - 1, :W].T
                head_sum[...] = heads[STEPS - 1, W:W + 1]
                tail[...] = tails[STEPS - 1, :W].T
                tail_sum[...] = tails[STEPS - 1, W:W + 1]
                for c in stores[:4]:
                    c.start()

        for p in range(N_PARTS):
            to_other(p).wait_send()
            wait_bytes(xrecv.at[s, :, :, lanes(p)], s_x.at[p])
            wait_bytes(xrecv.at[s, :, :, lanes(p)], s_xg.at[p])

        @pl.when(owner)
        def _():
            wait_bytes(zrecv.at[s], s_zg)
            wait_bytes(mine.at[:, pl.ds(0, (TILES - 1) * 128)], s_z)

        @pl.when(jnp.logical_not(owner))
        def _():
            wait_bytes(mine, s_z)

        for p in range(N_PARTS):
            to_core(p).wait()
            if COMPUTE:
                for j in range(*PARTS[p]):
                    at = slice(j * 128, (j + 1) * 128)
                    grad = total[s, :, :, at].reshape(W, 128)
                    new = rsum[:, at] + jnp.mean(grad * grad, axis=0, keepdims=True)
                    rsum[:, at] = new
                    part = relT[:, at] - LEARN_RATE * grad * lax.rsqrt(new)
                    relT[:, at] = part
                    relhl[:W, at], relhl[W:, at] = split(part)

                @pl.when(more)
                def _():
                    gather_relations(p)

                @pl.when(jnp.logical_not(more))
                def _():
                    for j in range(*PARTS[p]):
                        count = min(128, RELS - j * 128)
                        rel[j * 128:j * 128 + count] = relT[:, j * 128:(j + 1) * 128].T[:count]
                    stores[5 + p].start()

        if COMPUTE:
            @pl.when(more)
            def _():
                terms()
        return carry

    lax.fori_loop(0, STEPS, step, 0)

    rel_sum[...] = rsum[:, :RELS].reshape(RELS)
    stores[4].start()
    if not COMPUTE:
        for k, c in enumerate(stores):
            if k != 4:
                c.start()
    for c in stores:
        c.wait()


def write_out(*refs):
    count = (len(refs) - 2) // 3
    ins, outs, held, (s_read, s_write) = refs[:count], refs[count:2 * count], refs[2 * count:3 * count], refs[-2:]
    read = [pltpu.make_async_copy(ins[k], held[k], s_read.at[k]) for k in range(count)]
    write = [pltpu.make_async_copy(held[k], outs[k], s_write.at[k]) for k in range(count)]
    for c in read:
        c.start()
    for c, d in zip(read, write):
        c.wait()
        d.start()
    for d in write:
        d.wait()


def held():
    shapes = ((ROWS, W), (1, ROWS), (ROWS, W), (1, ROWS), (RELS, W), (RELS,))
    return tuple(jax.ShapeDtypeStruct(shape, F32) for shape in shapes)


def window(head, head_state, tail, tail_state, relations, relation_state, edge_heads, edge_rels, edge_tails, negatives):
    dma, vmem = pltpu.SemaphoreType.DMA, pltpu.VMEM
    in_hbm = pl.BlockSpec(memory_space=pltpu.HBM)
    return pl.pallas_call(
        kernel,
        out_shape=held(),
        in_specs=[in_hbm] * 10,
        out_specs=[in_hbm] * 6,
        scratch_shapes=[
            vmem((ROWS, W), F32),
            vmem((ROWS, W), F32),
            vmem((RELS, W), F32),
            vmem((STEPS, 1, EDGES), jnp.int32),
            vmem((STEPS, 1, EDGES), jnp.int32),
            vmem((STEPS, 1, EDGES), jnp.int32),
            vmem((STEPS, BLOCKS, NEG), jnp.int32),
            vmem((1, ROWS), F32),
            vmem((1, ROWS), F32),
            vmem((RELS,), F32),
            dma((10,)),
            vmem((STEPS, SLAB, ROWS), F32),
            vmem((2 * STEPS, SLAB, ROWS), F32),
            vmem((W, RPAD), F32),
            vmem((1, RPAD), F32),
            vmem((2 * W, RPAD), BF16),
            vmem((RPAD, EDGES), BF16),
            vmem((ROWS, EDGES), BF16),
            vmem((ROWS, EDGES), BF16),
            vmem((ROWS, EDGES), F32),
            vmem((W, EDGES), F32),
            vmem((W, EDGES), F32),
            vmem((W, EDGES), F32),
            vmem((ROWS, W), BF16),
            vmem((W, ROWS), BF16),
            vmem((W, EDGES), F32),
            vmem((1, EDGES), F32),
            vmem((W, EDGES), BF16),
            vmem((ROWS, EDGES), BF16),
            vmem((ROWS, EDGES), BF16),
            vmem((W, EDGES), F32),
            vmem((2, W, EDGES), BF16),
            vmem((2 * XY, 8, RPAD), F32),
            vmem((STEPS, 2 * XY, 8, RPAD), F32),
            vmem((STEPS, XY, 8, RPAD), F32),
            vmem((XY, 8, RPAD), F32),
            vmem((STEPS, N_OFF, 8, RPAD), F32),
            vmem((STEPS, NZ - 1, 8, 128), F32),
            vmem((8, RPAD), F32),
            dma((N_PARTS,)), dma((STEPS, N_PARTS)),
            dma((N_PARTS,)), dma((STEPS, N_PARTS)),
            dma, dma((STEPS,)),
            dma, dma((STEPS, N_PARTS)),
            dma((N_PARTS,)), dma((STEPS, N_PARTS)),
            dma((N_PARTS,)), dma((STEPS, N_PARTS)),
            dma, dma((STEPS,)),
            dma, dma((STEPS,)),
            dma, dma((STEPS,)),
        ],
        compiler_params=pltpu.CompilerParams(
            collective_id=0, has_side_effects=True, vmem_limit_bytes=VMEM_LIMIT
        ),
        name="window",
    )(
        head.reshape(ROWS, W),
        head_state.reshape(1, ROWS),
        tail.reshape(ROWS, W),
        tail_state.reshape(1, ROWS),
        relations,
        relation_state,
        edge_heads.reshape(STEPS, 1, EDGES),
        edge_rels.reshape(STEPS, 1, EDGES),
        edge_tails.reshape(STEPS, 1, EDGES),
        negatives.reshape(STEPS, BLOCKS, NEG),
    )


def body(*args):
    out = window(*args)
    dma, vmem = pltpu.SemaphoreType.DMA, pltpu.VMEM
    in_hbm = pl.BlockSpec(memory_space=pltpu.HBM)
    out = pl.pallas_call(
        write_out,
        out_shape=held(),
        in_specs=[in_hbm] * 6,
        out_specs=[in_hbm] * 6,
        scratch_shapes=[vmem(h.shape, F32) for h in held()] + [dma((6,)), dma((6,))],
        compiler_params=pltpu.CompilerParams(vmem_limit_bytes=VMEM_LIMIT),
        name="write_out",
    )(*out)
    return (
        out[0].reshape(1, 1, ROWS, W),
        out[1].reshape(1, 1, ROWS),
        out[2].reshape(1, 1, ROWS, W),
        out[3].reshape(1, 1, ROWS),
        out[4],
        out[5],
    )


def solution(mesh):
    slab, sums = P("lhs", "rhs", None, None), P("lhs", "rhs", None)
    return jax.shard_map(
        body,
        mesh=mesh,
        in_specs=(slab, sums, slab, sums, P(), P(), slab, slab, slab, P("lhs", "rhs", None, None, None)),
        out_specs=(slab, sums, slab, sums, P(), P()),
        check_vma=False,
    )
```

```python
import functools

import jax
import jax.numpy as jnp
from jax import lax
from jax.experimental import pallas as pl
from jax.experimental.pallas import tpu as pltpu
from jax.sharding import PartitionSpec as P

LEARN_RATE = 0.1
MESH = pl.DeviceIdType.MESH
F32, BF16 = jnp.float32, jnp.bfloat16

NX, NY, NZ = 4, 4, 16
N_LHS, N_RHS = 2 * NY * 2, NZ * 2
XY = NX * NY
W, HALF, ROWS, EDGES, RELS, STEPS = 256, 128, 512, 512, 1300, 3
BLOCKS, NEG = 4, 256
BLOCK = EDGES // BLOCKS
TILES = -(-RELS // 128)
RPAD = TILES * 128
SLAB = W + 8
HALVES = (pl.ds(0, 136), pl.ds(136, SLAB - 136))

PARTS = ((0, 6), (6, 11))
N_PARTS = len(PARTS)
OFFS = sorted(
    [(dx, dy) for dx in range(NX) for dy in range(NY) if (dx, dy) != (0, 0)],
    key=lambda o: (min(o[0], NX - o[0]) + min(o[1], NY - o[1])),
)
N_OFF = len(OFFS)
OWN = [j * NZ // TILES for j in range(TILES)]
COMPUTE = True
MOVE = True
VMEM_LIMIT = 60 * 2**20


def coords():
    a, b = lax.axis_index("lhs"), lax.axis_index("rhs")
    core, y, xh = lax.rem(a, 2), lax.rem(lax.div(a, 2), NY), lax.div(a, 2 * NY)
    return xh * 2 + lax.rem(b, 2), y, lax.div(b, 2), core


def device(x, y, z, core):
    return ((lax.div(x, 2) * NY + y) * 2 + core, z * 2 + lax.rem(x, 2))


def nn(a, b):
    return jnp.dot(a, b, preferred_element_type=F32)


def nt(a, b):
    return lax.dot_general(a, b, (((1,), (1,)), ((), ())), preferred_element_type=F32)


def split(x):
    hi = x.astype(BF16)
    return hi, (x - hi.astype(F32)).astype(BF16)


def one_hot(index, count):
    place = lax.broadcasted_iota(jnp.int32, (count, index.shape[1]), 0)
    return jnp.where(place == index, 1.0, 0.0).astype(BF16)


def remote(src, dst, send, recv, to):
    return pltpu.make_async_remote_copy(
        src_ref=src, dst_ref=dst, send_sem=send, recv_sem=recv, device_id=to, device_id_type=MESH
    )


def wait_bytes(like, sem):
    pltpu.make_async_copy(like, like, sem).wait()


def kernel(
    head_in, head_sum_in, tail_in, tail_sum_in, rel_in, rel_sum_in, eh_in, er_in, et_in, ng_in,
    head_out, head_sum_out, tail_out, tail_sum_out, rel_out, rel_sum_out,
    head, tail, rel, eh, er, et, ng, head_sum, tail_sum, rel_sum, s_in,
    heads, tails, relT, rsum, relhl, oh_r, oh_h, oh_t, cnt,
    hT, tT, rT, tb, tbT, q, dpos, qb, phi, plo, gq, grhl,
    g, total, crecv, acc, xrecv, zrecv, mine,
    s_c, r_c, s_x, r_x, s_z, r_z, s_zg, r_zg, s_xg, r_xg, s_cg, r_cg, s_h, r_h, s_t, r_t, r_tb,
):
    x, y, z, core = coords()
    me = x * NY + y
    lo, other = core * XY, (1 - core) * XY
    a, b = lax.axis_index("lhs"), lax.axis_index("rhs")
    partner = device(x, y, z, 1 - core)
    head_to, head_from = (lax.rem(a + 1, N_LHS), b), (lax.rem(a + N_LHS - 1, N_LHS), b)
    plane = []
    for dx, dy in OFFS:
        tx, ty = lax.rem(x + dx, NX), lax.rem(y + dy, NY)
        plane.append((device(tx, ty, z, core), tx * NY + ty))

    barrier = pltpu.get_barrier_semaphore()
    peers = [device(x, y, lax.rem(z + dz, NZ), core) for dz in range(1, NZ)]
    peers += [d for d, _ in plane] + [partner, head_to, head_from]
    for d in peers:
        pl.semaphore_signal(barrier, inc=1, device_id=d, device_id_type=MESH)

    loads = [
        (er_in, er), (eh_in, eh), (et_in, et), (ng_in, ng), (head_in, head), (tail_in, tail), (rel_in, rel),
        (head_sum_in, head_sum), (tail_sum_in, tail_sum), (rel_sum_in, rel_sum),
    ]
    loads = [pltpu.make_async_copy(src, dst, s_in.at[k]) for k, (src, dst) in enumerate(loads)]
    for c in loads:
        c.start()

    stores = [
        (head, head_out), (head_sum, head_sum_out), (tail, tail_out), (tail_sum, tail_sum_out),
        (rel_sum, rel_sum_out),
    ]
    for first, last in PARTS:
        rows = pl.ds(first * 128, min(last * 128, RELS) - first * 128)
        stores.append((rel.at[rows], rel_out.at[rows]))
    stores = [pltpu.make_async_copy(src, dst, s_in.at[k]) for k, (src, dst) in enumerate(stores)]

    def prep_index(s):
        oh_r[...] = one_hot(er[s], RPAD)
        oh_h[...] = one_hot(eh[s], ROWS)
        oh_t[...] = one_hot(et[s], ROWS)
        ones = jnp.ones((NEG, BLOCK), BF16)
        for k in range(BLOCKS):
            cnt[:, k * BLOCK:(k + 1) * BLOCK] = nn(one_hot(ng[s, k:k + 1], ROWS), ones)

    def gather(wide, hot):
        both = nn(jnp.concatenate(split(wide), axis=0), hot)
        return both[:W] + both[W:]

    def prep_head(s):
        hT[...] = gather(heads[s, :W], oh_h[...])

    def prep_tail(s):
        slab = tails[s, :W]
        tT[...] = gather(slab, oh_t[...])
        tbT[...] = slab.astype(BF16)
        tb[...] = slab.T.astype(BF16)

    def update(slab, total_grad):
        new = slab[W:W + 1] + jnp.mean(total_grad * total_grad, axis=0, keepdims=True)
        slab[W:W + 1] = new
        slab[:W] = slab[:W] - LEARN_RATE * total_grad * lax.rsqrt(new)

    def lanes(p):
        return pl.ds(PARTS[p][0] * 128, (PARTS[p][1] - PARTS[p][0]) * 128)

    def relation_grad(k, p):
        both = nt(grhl[k], oh_r[lanes(p)])
        g[pl.ds(k * XY, XY), :, lanes(p)] = (both[:HALF] + both[HALF:]).reshape(XY, 8, -1)

    def gather_relations(p):
        both = nn(relhl[:, lanes(p)], oh_r[lanes(p)])
        part = both[:W] + both[W:]
        rT[...] = part if p == 0 else rT[...] + part

    def terms():
        r_re, r_im = rT[:HALF], rT[HALF:]
        h_re, h_im = hT[:HALF], hT[HALF:]
        q_re, q_im = h_re * r_re - h_im * r_im, h_re * r_im + h_im * r_re
        q[:HALF], q[HALF:] = q_re, q_im
        pos = jnp.sum(q_re * tT[:HALF] + q_im * tT[HALF:], axis=0, keepdims=True)
        dp = -jax.nn.sigmoid(-pos)
        dpos[...] = dp
        qb[:HALF], qb[HALF:] = q_re.astype(BF16), q_im.astype(BF16)
        scores = nn(tb[...], qb[...])
        dneg = (jax.nn.sigmoid(scores) * (1.0 / NEG)).astype(BF16)
        phi[...], plo[...] = split(dneg.astype(F32) * cnt[...])
        grad_q = dp * tT[...] + (nn(tbT[...], phi[...]) + nn(tbT[...], plo[...]))
        gq[...] = grad_q
        g_re, g_im = grad_q[:HALF], grad_q[HALF:]
        for k, term in enumerate((g_re * h_re + g_im * h_im, g_im * h_re - g_re * h_im)):
            grhl[k, :HALF], grhl[k, HALF:] = split(term)
        relation_grad(1 - core, 0)

    def head_update(s):
        g_re, g_im = gq[:HALF], gq[HALF:]
        r_re, r_im = rT[:HALF], rT[HALF:]
        term = jnp.concatenate([g_re * r_re + g_im * r_im, g_im * r_re - g_re * r_im], axis=0)
        both = nt(jnp.concatenate(split(term), axis=0), oh_h[...])
        update(heads.at[s], both[:W] + both[W:])

    def tail_update(s):
        term = dpos[...] * q[...]
        both = nt(jnp.concatenate(split(term), axis=0), oh_t[...])
        neg = nt(qb[...], phi[...]) + nt(qb[...], plo[...])
        update(tails.at[s], both[:W] + both[W:] + neg)

    if COMPUTE:
        for c in loads[:4]:
            c.wait()
        prep_index(0)
        for c in loads[4:]:
            c.wait()
        rsum[...] = jnp.ones_like(rsum)
        rsum[:, :RELS] = rel_sum[...].reshape(1, RELS)
        heads[0, :W] = head[...].T
        heads[0, W:W + 1] = head_sum[...]
        prep_head(0)
        tails[0, :W] = tail[...].T
        tails[0, W:W + 1] = tail_sum[...]
        prep_tail(0)
        for j in range(TILES):
            at = slice(j * 128, (j + 1) * 128)
            count = min(128, RELS - j * 128)
            part = rel[j * 128:j * 128 + count]
            if count < 128:
                part = jnp.concatenate([part, jnp.zeros((128 - count, W), F32)], axis=0)
            part = part.T
            relT[:, at] = part
            relhl[:W, at], relhl[W:, at] = split(part)
        for p in range(N_PARTS):
            gather_relations(p)
        terms()
    else:
        for c in loads:
            c.wait()
    pl.semaphore_wait(barrier, len(peers))

    x_lo = lax.rem(b, 2)
    tile = z - lax.div(z, 3)
    owner = jnp.logical_or(z == 0, lax.rem(z, 3) != 0)

    def step(s, carry):
        more = s < STEPS - 1
        move_head = [
            remote(heads.at[s, rows], heads.at[s + 1, rows], s_h.at[k], r_h.at[s, k], head_to)
            for k, rows in enumerate(HALVES)
        ]
        along_z = (a, lax.rem(b + 2, N_RHS))
        along_x = (a, b + 1 - 2 * x_lo)
        first, second = HALVES
        here, there, between = tails.at[s], tails.at[s + 1], tails.at[STEPS + s]
        odd_moves = (
            remote(here.at[first], between.at[first], s_t.at[0], r_tb.at[s], along_z),
            remote(here.at[second], between.at[second], s_t.at[1], r_tb.at[s], along_x),
            remote(between.at[first], there.at[first], s_t.at[2], r_t.at[s, 0], along_x),
        )
        even_moves = (
            remote(here.at[first], there.at[first], s_t.at[0], r_t.at[s, 0], along_x),
            remote(here.at[second], there.at[second], s_t.at[1], r_t.at[s, 1], along_x),
            remote(between.at[second], there.at[second], s_t.at[2], r_t.at[s, 1], along_z),
        )

        def to_other(p):
            return remote(
                g.at[pl.ds(other, XY), :, lanes(p)], crecv.at[s, :, :, lanes(p)], s_c.at[p], r_c.at[s, p], partner
            )

        def to_plane(p):
            to_other(p).wait_recv()
            for k, (d, t) in enumerate(plane):
                acc[t, :, lanes(p)] = g[lo + t, :, lanes(p)] + crecv[s, t, :, lanes(p)]
                remote(acc.at[t, :, lanes(p)], xrecv.at[s, k, :, lanes(p)], s_x.at[p], r_x.at[s, p], d).start()
            mine[:, lanes(p)] = g[lo + me, :, lanes(p)] + crecv[s, me, :, lanes(p)]

        to_other(0).start()
        if COMPUTE:
            relation_grad(1 - core, 1)
        to_other(1).start()
        if COMPUTE:
            relation_grad(core, 0)
        to_plane(0)
        if COMPUTE:
            relation_grad(core, 1)
        to_plane(1)

        if COMPUTE:
            tail_update(s)
        if MOVE:
            @pl.when(jnp.logical_and(more, x_lo == 1))
            def _():
                odd_moves[0].start()
        if COMPUTE:
            head_update(s)

        for p in range(N_PARTS):
            wait_bytes(xrecv.at[s, :, :, lanes(p)], r_x.at[s, p])
            part = mine[:, lanes(p)]
            for k in range(N_OFF):
                part = part + xrecv[s, k, :, lanes(p)]
            mine[:, lanes(p)] = part
            for j in range(*PARTS[p]):
                @pl.when(z != OWN[j])
                def _():
                    remote(
                        mine.at[:, pl.ds(j * 128, 128)], zrecv.at[s, lax.rem(z - OWN[j] + NZ, NZ) - 1],
                        s_z, r_z.at[s], device(x, y, OWN[j], core),
                    ).start()

        if MOVE:
            @pl.when(more)
            def _():
                @pl.when(x_lo == 1)
                def _():
                    odd_moves[1].start()

                @pl.when(x_lo == 0)
                def _():
                    even_moves[0].start()

                move_head[0].start()

        @pl.when(owner)
        def _():
            wait_bytes(zrecv.at[s], r_z.at[s])
            at = pl.ds(pl.multiple_of(tile * 128, 128), 128)
            part = mine[:, at]
            for k in range(NZ - 1):
                part = part + zrecv[s, k]
            total[s, lo + me, :, at] = part
            ref = total.at[s, lo + me, :, at]
            which = jnp.where(tile >= PARTS[0][1], 1, 0)
            for k in sorted(range(1, NZ), key=lambda d: -min(d, NZ - d)):
                to = device(x, y, lax.rem(z + k, NZ), core)
                remote(ref, ref, s_zg, r_zg.at[s, which], to).start()

        if MOVE:
            @pl.when(more)
            def _():
                @pl.when(x_lo == 1)
                def _():
                    odd_moves[0].wait_recv()
                    odd_moves[2].start()

                @pl.when(x_lo == 0)
                def _():
                    even_moves[1].start()

                move_head[1].start()

        def to_core(p):
            ref = total.at[s, pl.ds(lo, XY), :, lanes(p)]
            return remote(ref, ref, s_cg.at[p], r_cg.at[s, p], partner)

        for p in range(N_PARTS):
            first, last = PARTS[p]
            mine_too = jnp.logical_and(owner, jnp.logical_and(tile >= first, tile < last))

            @pl.when(mine_too)
            def _():
                wait_bytes(mine.at[:, pl.ds(0, (last - first - 1) * 128)], r_zg.at[s, p])

            @pl.when(jnp.logical_not(mine_too))
            def _():
                wait_bytes(mine.at[:, pl.ds(0, (last - first) * 128)], r_zg.at[s, p])

            ref = total.at[s, lo + me, :, lanes(p)]
            for d, _ in plane:
                remote(ref, ref, s_xg.at[p], r_xg.at[s, p], d).start()

        if MOVE:
            @pl.when(jnp.logical_and(more, x_lo == 0))
            def _():
                odd_moves[1].wait_recv()
                even_moves[2].start()
        if COMPUTE:
            @pl.when(more)
            def _():
                prep_index(s + 1)

        wait_bytes(xrecv.at[s, :, :, lanes(0)], r_xg.at[s, 0])
        to_core(0).start()

        @pl.when(more)
        def _():
            if MOVE:
                for c in move_head:
                    c.wait()
            if COMPUTE:
                prep_head(s + 1)

        wait_bytes(xrecv.at[s, :, :, lanes(1)], r_xg.at[s, 1])
        to_core(1).start()

        @pl.when(more)
        def _():
            if MOVE:
                @pl.when(x_lo == 1)
                def _():
                    for c in odd_moves:
                        c.wait_send()

                @pl.when(x_lo == 0)
                def _():
                    for c in even_moves:
                        c.wait_send()

                even_moves[0].wait_recv()
                even_moves[1].wait_recv()
            if COMPUTE:
                prep_tail(s + 1)

        if COMPUTE:
            @pl.when(jnp.logical_not(more))
            def _():
                head[...] = heads[STEPS - 1, :W].T
                head_sum[...] = heads[STEPS - 1, W:W + 1]
                tail[...] = tails[STEPS - 1, :W].T
                tail_sum[...] = tails[STEPS - 1, W:W + 1]
                for c in stores[:4]:
                    c.start()

        for p in range(N_PARTS):
            to_other(p).wait_send()
            wait_bytes(xrecv.at[s, :, :, lanes(p)], s_x.at[p])
            wait_bytes(xrecv.at[s, :, :, lanes(p)], s_xg.at[p])

        @pl.when(owner)
        def _():
            wait_bytes(zrecv.at[s], s_zg)
            wait_bytes(mine.at[:, pl.ds(0, (TILES - 1) * 128)], s_z)

        @pl.when(jnp.logical_not(owner))
        def _():
            wait_bytes(mine, s_z)

        for p in range(N_PARTS):
            to_core(p).wait()
            if COMPUTE:
                for j in range(*PARTS[p]):
                    at = slice(j * 128, (j + 1) * 128)
                    grad = total[s, :, :, at].reshape(W, 128)
                    new = rsum[:, at] + jnp.mean(grad * grad, axis=0, keepdims=True)
                    rsum[:, at] = new
                    part = relT[:, at] - LEARN_RATE * grad * lax.rsqrt(new)
                    relT[:, at] = part
                    relhl[:W, at], relhl[W:, at] = split(part)

                @pl.when(more)
                def _():
                    gather_relations(p)

                @pl.when(jnp.logical_not(more))
                def _():
                    for j in range(*PARTS[p]):
                        count = min(128, RELS - j * 128)
                        rel[j * 128:j * 128 + count] = relT[:, j * 128:(j + 1) * 128].T[:count]
                    stores[5 + p].start()

        if COMPUTE:
            @pl.when(more)
            def _():
                terms()
        return carry

    lax.fori_loop(0, STEPS, step, 0)

    rel_sum[...] = rsum[:, :RELS].reshape(RELS)
    stores[4].start()
    if not COMPUTE:
        for k, c in enumerate(stores):
            if k != 4:
                c.start()
    for c in stores:
        c.wait()


PIECES = [(k, pl.ds(n, 256)) for k in (0, 2) for n in (0, 256)] + [(4, pl.ds(n, min(256, RELS - n))) for n in range(0, RELS, 256)]
PIECES += [(k, slice(None)) for k in (1, 3, 5)]


def write_out(*refs):
    ins, outs, kept, (s_read, s_write) = refs[:6], refs[6:12], refs[12:18], refs[18:]
    read, write = [], []
    for n, (k, rows) in enumerate(PIECES):
        src, mid, dst = ins[k], kept[k], outs[k]
        if not isinstance(rows, slice):
            src, mid, dst = src.at[rows], mid.at[rows], dst.at[rows]
        read.append(pltpu.make_async_copy(src, mid, s_read.at[n]))
        write.append(pltpu.make_async_copy(mid, dst, s_write.at[n]))
    for c in read:
        c.start()
    for c, d in zip(read, write):
        c.wait()
        d.start()
    for d in write:
        d.wait()


def held():
    shapes = ((ROWS, W), (1, ROWS), (ROWS, W), (1, ROWS), (RELS, W), (RELS,))
    return tuple(jax.ShapeDtypeStruct(shape, F32) for shape in shapes)


def window(head, head_state, tail, tail_state, relations, relation_state, edge_heads, edge_rels, edge_tails, negatives):
    dma, vmem = pltpu.SemaphoreType.DMA, pltpu.VMEM
    in_hbm = pl.BlockSpec(memory_space=pltpu.HBM)
    return pl.pallas_call(
        kernel,
        out_shape=held(),
        in_specs=[in_hbm] * 10,
        out_specs=[in_hbm] * 6,
        scratch_shapes=[
            vmem((ROWS, W), F32),
            vmem((ROWS, W), F32),
            vmem((RELS, W), F32),
            vmem((STEPS, 1, EDGES), jnp.int32),
            vmem((STEPS, 1, EDGES), jnp.int32),
            vmem((STEPS, 1, EDGES), jnp.int32),
            vmem((STEPS, BLOCKS, NEG), jnp.int32),
            vmem((1, ROWS), F32),
            vmem((1, ROWS), F32),
            vmem((RELS,), F32),
            dma((10,)),
            vmem((STEPS, SLAB, ROWS), F32),
            vmem((2 * STEPS, SLAB, ROWS), F32),
            vmem((W, RPAD), F32),
            vmem((1, RPAD), F32),
            vmem((2 * W, RPAD), BF16),
            vmem((RPAD, EDGES), BF16),
            vmem((ROWS, EDGES), BF16),
            vmem((ROWS, EDGES), BF16),
            vmem((ROWS, EDGES), F32),
            vmem((W, EDGES), F32),
            vmem((W, EDGES), F32),
            vmem((W, EDGES), F32),
            vmem((ROWS, W), BF16),
            vmem((W, ROWS), BF16),
            vmem((W, EDGES), F32),
            vmem((1, EDGES), F32),
            vmem((W, EDGES), BF16),
            vmem((ROWS, EDGES), BF16),
            vmem((ROWS, EDGES), BF16),
            vmem((W, EDGES), F32),
            vmem((2, W, EDGES), BF16),
            vmem((2 * XY, 8, RPAD), F32),
            vmem((STEPS, 2 * XY, 8, RPAD), F32),
            vmem((STEPS, XY, 8, RPAD), F32),
            vmem((XY, 8, RPAD), F32),
            vmem((STEPS, N_OFF, 8, RPAD), F32),
            vmem((STEPS, NZ - 1, 8, 128), F32),
            vmem((8, RPAD), F32),
            dma((N_PARTS,)), dma((STEPS, N_PARTS)),
            dma((N_PARTS,)), dma((STEPS, N_PARTS)),
            dma, dma((STEPS,)),
            dma, dma((STEPS, N_PARTS)),
            dma((N_PARTS,)), dma((STEPS, N_PARTS)),
            dma((N_PARTS,)), dma((STEPS, N_PARTS)),
            dma((2,)), dma((STEPS, 2)),
            dma((3,)), dma((STEPS, 2)), dma((STEPS,)),
        ],
        compiler_params=pltpu.CompilerParams(
            collective_id=0, has_side_effects=True, vmem_limit_bytes=VMEM_LIMIT
        ),
        name="window",
    )(
        head.reshape(ROWS, W),
        head_state.reshape(1, ROWS),
        tail.reshape(ROWS, W),
        tail_state.reshape(1, ROWS),
        relations,
        relation_state,
        edge_heads.reshape(STEPS, 1, EDGES),
        edge_rels.reshape(STEPS, 1, EDGES),
        edge_tails.reshape(STEPS, 1, EDGES),
        negatives.reshape(STEPS, BLOCKS, NEG),
    )


def body(*args):
    out = window(*args)
    dma, vmem = pltpu.SemaphoreType.DMA, pltpu.VMEM
    in_hbm = pl.BlockSpec(memory_space=pltpu.HBM)
    out = pl.pallas_call(
        write_out,
        out_shape=held(),
        in_specs=[in_hbm] * 6,
        out_specs=[in_hbm] * 6,
        scratch_shapes=[vmem(h.shape, F32) for h in held()] + [dma((len(PIECES),))] * 2,
        compiler_params=pltpu.CompilerParams(vmem_limit_bytes=VMEM_LIMIT),
        name="write_out",
    )(*out)
    return (
        out[0].reshape(1, 1, ROWS, W),
        out[1].reshape(1, 1, ROWS),
        out[2].reshape(1, 1, ROWS, W),
        out[3].reshape(1, 1, ROWS),
        out[4],
        out[5],
    )


def solution(mesh):
    slab, sums = P("lhs", "rhs", None, None), P("lhs", "rhs", None)
    return jax.shard_map(
        body,
        mesh=mesh,
        in_specs=(slab, sums, slab, sums, P(), P(), slab, slab, slab, P("lhs", "rhs", None, None, None)),
        out_specs=(slab, sums, slab, sums, P(), P()),
        check_vma=False,
    )
```

```python
import functools

import jax
import jax.numpy as jnp
from jax import lax
from jax.experimental import pallas as pl
from jax.experimental.pallas import tpu as pltpu
from jax.sharding import PartitionSpec as P

LEARN_RATE = 0.1
MESH = pl.DeviceIdType.MESH
F32, BF16 = jnp.float32, jnp.bfloat16

NX, NY, NZ = 4, 4, 16
N_LHS, N_RHS = 2 * NY * 2, NZ * 2
XY = NX * NY
W, HALF, ROWS, EDGES, RELS, STEPS = 256, 128, 512, 512, 1300, 3
BLOCKS, NEG = 4, 256
BLOCK = EDGES // BLOCKS
TILES = -(-RELS // 128)
RPAD = TILES * 128
SLAB = W + 8
HALVES = (pl.ds(0, 136), pl.ds(136, SLAB - 136))

PARTS = ((0, 6), (6, 11))
N_PARTS = len(PARTS)
OFFS = sorted(
    [(dx, dy) for dx in range(NX) for dy in range(NY) if (dx, dy) != (0, 0)],
    key=lambda o: -(min(o[0], NX - o[0]) + min(o[1], NY - o[1])),
)
N_OFF = len(OFFS)
OWN = [j * NZ // TILES for j in range(TILES)]
COMPUTE = True
MOVE = True
VMEM_LIMIT = 60 * 2**20


def coords():
    a, b = lax.axis_index("lhs"), lax.axis_index("rhs")
    core, y, xh = lax.rem(a, 2), lax.rem(lax.div(a, 2), NY), lax.div(a, 2 * NY)
    return xh * 2 + lax.rem(b, 2), y, lax.div(b, 2), core


def device(x, y, z, core):
    return ((lax.div(x, 2) * NY + y) * 2 + core, z * 2 + lax.rem(x, 2))


def nn(a, b):
    return jnp.dot(a, b, preferred_element_type=F32)


def nt(a, b):
    return lax.dot_general(a, b, (((1,), (1,)), ((), ())), preferred_element_type=F32)


def split(x):
    hi = x.astype(BF16)
    return hi, (x - hi.astype(F32)).astype(BF16)


def one_hot(index, count):
    place = lax.broadcasted_iota(jnp.int32, (count, index.shape[1]), 0)
    return jnp.where(place == index, 1.0, 0.0).astype(BF16)


def remote(src, dst, send, recv, to):
    return pltpu.make_async_remote_copy(
        src_ref=src, dst_ref=dst, send_sem=send, recv_sem=recv, device_id=to, device_id_type=MESH
    )


def wait_bytes(like, sem):
    pltpu.make_async_copy(like, like, sem).wait()


def kernel(
    head_in, head_sum_in, tail_in, tail_sum_in, rel_in, rel_sum_in, eh_in, er_in, et_in, ng_in,
    head_out, head_sum_out, tail_out, tail_sum_out, rel_out, rel_sum_out,
    head, tail, rel, eh, er, et, ng, head_sum, tail_sum, rel_sum, s_in,
    heads, tails, relT, rsum, relhl, oh_r, oh_h, oh_t, cnt,
    hT, tT, rT, tb, tbT, q, dpos, qb, phi, plo, gq, grhl,
    g, total, crecv, acc, xrecv, zrecv, mine,
    s_c, r_c, s_x, r_x, s_z, r_z, s_zg, r_zg, s_xg, r_xg, s_cg, r_cg, s_h, r_h, s_t, r_t, r_tb,
):
    x, y, z, core = coords()
    me = x * NY + y
    lo, other = core * XY, (1 - core) * XY
    a, b = lax.axis_index("lhs"), lax.axis_index("rhs")
    partner = device(x, y, z, 1 - core)
    head_to, head_from = (lax.rem(a + 1, N_LHS), b), (lax.rem(a + N_LHS - 1, N_LHS), b)
    plane = []
    sign = 1 - 2 * lax.rem(x + y, 2)
    for dx, dy in OFFS:
        ex, ey = dx + core * (dy - dx), dy + core * (dx - dy)
        tx, ty = lax.rem(x + sign * ex + NX, NX), lax.rem(y + sign * ey + NY, NY)
        plane.append((device(tx, ty, z, core), tx * NY + ty))

    barrier = pltpu.get_barrier_semaphore()
    peers = [device(x, y, lax.rem(z + dz, NZ), core) for dz in range(1, NZ)]
    peers += [d for d, _ in plane] + [partner, head_to, head_from]
    for d in peers:
        pl.semaphore_signal(barrier, inc=1, device_id=d, device_id_type=MESH)

    loads = [
        (er_in, er), (eh_in, eh), (et_in, et), (ng_in, ng), (head_in, head), (tail_in, tail), (rel_in, rel),
        (head_sum_in, head_sum), (tail_sum_in, tail_sum), (rel_sum_in, rel_sum),
    ]
    loads = [pltpu.make_async_copy(src, dst, s_in.at[k]) for k, (src, dst) in enumerate(loads)]
    for c in loads:
        c.start()

    stores = [
        (head, head_out), (head_sum, head_sum_out), (tail, tail_out), (tail_sum, tail_sum_out),
        (rel_sum, rel_sum_out),
    ]
    for first, last in PARTS:
        rows = pl.ds(first * 128, min(last * 128, RELS) - first * 128)
        stores.append((rel.at[rows], rel_out.at[rows]))
    stores = [pltpu.make_async_copy(src, dst, s_in.at[k]) for k, (src, dst) in enumerate(stores)]

    def prep_index(s):
        oh_r[...] = one_hot(er[s], RPAD)
        oh_h[...] = one_hot(eh[s], ROWS)
        oh_t[...] = one_hot(et[s], ROWS)
        ones = jnp.ones((NEG, BLOCK), BF16)
        for k in range(BLOCKS):
            cnt[:, k * BLOCK:(k + 1) * BLOCK] = nn(one_hot(ng[s, k:k + 1], ROWS), ones)

    def gather(wide, hot):
        both = nn(jnp.concatenate(split(wide), axis=0), hot)
        return both[:W] + both[W:]

    def prep_head(s):
        hT[...] = gather(heads[s, :W], oh_h[...])

    def prep_tail(s):
        slab = tails[s, :W]
        tT[...] = gather(slab, oh_t[...])
        tbT[...] = slab.astype(BF16)
        tb[...] = slab.T.astype(BF16)

    def update(slab, total_grad):
        new = slab[W:W + 1] + jnp.mean(total_grad * total_grad, axis=0, keepdims=True)
        slab[W:W + 1] = new
        slab[:W] = slab[:W] - LEARN_RATE * total_grad * lax.rsqrt(new)

    def lanes(p):
        return pl.ds(PARTS[p][0] * 128, (PARTS[p][1] - PARTS[p][0]) * 128)

    def relation_grad(k, p):
        both = nt(grhl[k], oh_r[lanes(p)])
        g[pl.ds(k * XY, XY), :, lanes(p)] = (both[:HALF] + both[HALF:]).reshape(XY, 8, -1)

    def gather_relations(p):
        both = nn(relhl[:, lanes(p)], oh_r[lanes(p)])
        part = both[:W] + both[W:]
        rT[...] = part if p == 0 else rT[...] + part

    def terms():
        r_re, r_im = rT[:HALF], rT[HALF:]
        h_re, h_im = hT[:HALF], hT[HALF:]
        q_re, q_im = h_re * r_re - h_im * r_im, h_re * r_im + h_im * r_re
        q[:HALF], q[HALF:] = q_re, q_im
        pos = jnp.sum(q_re * tT[:HALF] + q_im * tT[HALF:], axis=0, keepdims=True)
        dp = -jax.nn.sigmoid(-pos)
        dpos[...] = dp
        qb[:HALF], qb[HALF:] = q_re.astype(BF16), q_im.astype(BF16)
        scores = nn(tb[...], qb[...])
        dneg = (jax.nn.sigmoid(scores) * (1.0 / NEG)).astype(BF16)
        phi[...], plo[...] = split(dneg.astype(F32) * cnt[...])
        grad_q = dp * tT[...] + (nn(tbT[...], phi[...]) + nn(tbT[...], plo[...]))
        gq[...] = grad_q
        g_re, g_im = grad_q[:HALF], grad_q[HALF:]
        for k, term in enumerate((g_re * h_re + g_im * h_im, g_im * h_re - g_re * h_im)):
            grhl[k, :HALF], grhl[k, HALF:] = split(term)
        relation_grad(1 - core, 0)

    def head_update(s):
        g_re, g_im = gq[:HALF], gq[HALF:]
        r_re, r_im = rT[:HALF], rT[HALF:]
        term = jnp.concatenate([g_re * r_re + g_im * r_im, g_im * r_re - g_re * r_im], axis=0)
        both = nt(jnp.concatenate(split(term), axis=0), oh_h[...])
        update(heads.at[s], both[:W] + both[W:])

    def tail_update(s):
        term = dpos[...] * q[...]
        both = nt(jnp.concatenate(split(term), axis=0), oh_t[...])
        neg = nt(qb[...], phi[...]) + nt(qb[...], plo[...])
        update(tails.at[s], both[:W] + both[W:] + neg)

    if COMPUTE:
        for c in loads[:4]:
            c.wait()
        prep_index(0)
        for c in loads[4:]:
            c.wait()
        rsum[...] = jnp.ones_like(rsum)
        rsum[:, :RELS] = rel_sum[...].reshape(1, RELS)
        heads[0, :W] = head[...].T
        heads[0, W:W + 1] = head_sum[...]
        prep_head(0)
        tails[0, :W] = tail[...].T
        tails[0, W:W + 1] = tail_sum[...]
        prep_tail(0)
        for j in range(TILES):
            at = slice(j * 128, (j + 1) * 128)
            count = min(128, RELS - j * 128)
            part = rel[j * 128:j * 128 + count]
            if count < 128:
                part = jnp.concatenate([part, jnp.zeros((128 - count, W), F32)], axis=0)
            part = part.T
            relT[:, at] = part
            relhl[:W, at], relhl[W:, at] = split(part)
        for p in range(N_PARTS):
            gather_relations(p)
        terms()
    else:
        for c in loads:
            c.wait()
    pl.semaphore_wait(barrier, len(peers))

    x_lo = lax.rem(b, 2)
    tile = z - lax.div(z, 3)
    owner = jnp.logical_or(z == 0, lax.rem(z, 3) != 0)

    def step(s, carry):
        more = s < STEPS - 1
        move_head = [
            remote(heads.at[s, rows], heads.at[s + 1, rows], s_h.at[k], r_h.at[s, k], head_to)
            for k, rows in enumerate(HALVES)
        ]
        along_z = (a, lax.rem(b + 2, N_RHS))
        along_x = (a, b + 1 - 2 * x_lo)
        first, second = HALVES
        here, there, between = tails.at[s], tails.at[s + 1], tails.at[STEPS + s]
        odd_moves = (
            remote(here.at[first], between.at[first], s_t.at[0], r_tb.at[s], along_z),
            remote(here.at[second], between.at[second], s_t.at[1], r_tb.at[s], along_x),
            remote(between.at[first], there.at[first], s_t.at[2], r_t.at[s, 0], along_x),
        )
        even_moves = (
            remote(here.at[first], there.at[first], s_t.at[0], r_t.at[s, 0], along_x),
            remote(here.at[second], there.at[second], s_t.at[1], r_t.at[s, 1], along_x),
            remote(between.at[second], there.at[second], s_t.at[2], r_t.at[s, 1], along_z),
        )

        def to_other(p):
            return remote(
                g.at[pl.ds(other, XY), :, lanes(p)], crecv.at[s, :, :, lanes(p)], s_c.at[p], r_c.at[s, p], partner
            )

        def to_plane(p):
            to_other(p).wait_recv()
            for k, (d, t) in enumerate(plane):
                acc[t, :, lanes(p)] = g[lo + t, :, lanes(p)] + crecv[s, t, :, lanes(p)]
                remote(acc.at[t, :, lanes(p)], xrecv.at[s, k, :, lanes(p)], s_x.at[p], r_x.at[s, p], d).start()
            mine[:, lanes(p)] = g[lo + me, :, lanes(p)] + crecv[s, me, :, lanes(p)]

        to_other(0).start()
        if COMPUTE:
            relation_grad(1 - core, 1)
        to_other(1).start()
        if COMPUTE:
            relation_grad(core, 0)
        to_plane(0)
        if COMPUTE:
            relation_grad(core, 1)
        to_plane(1)

        if COMPUTE:
            tail_update(s)
        if MOVE:
            @pl.when(jnp.logical_and(more, x_lo == 1))
            def _():
                odd_moves[0].start()
        if COMPUTE:
            head_update(s)

        for p in range(N_PARTS):
            wait_bytes(xrecv.at[s, :, :, lanes(p)], r_x.at[s, p])
            part = mine[:, lanes(p)]
            for k in range(N_OFF):
                part = part + xrecv[s, k, :, lanes(p)]
            mine[:, lanes(p)] = part
            for j in range(*PARTS[p]):
                @pl.when(z != OWN[j])
                def _():
                    remote(
                        mine.at[:, pl.ds(j * 128, 128)], zrecv.at[s, lax.rem(z - OWN[j] + NZ, NZ) - 1],
                        s_z, r_z.at[s], device(x, y, OWN[j], core),
                    ).start()

        if MOVE:
            @pl.when(more)
            def _():
                @pl.when(x_lo == 1)
                def _():
                    odd_moves[1].start()
                    odd_moves[0].wait_recv()
                    odd_moves[2].start()

                @pl.when(x_lo == 0)
                def _():
                    even_moves[0].start()
                    even_moves[1].start()

                for c in move_head:
                    c.start()

        @pl.when(owner)
        def _():
            wait_bytes(zrecv.at[s], r_z.at[s])
            at = pl.ds(pl.multiple_of(tile * 128, 128), 128)
            part = mine[:, at]
            for k in range(NZ - 1):
                part = part + zrecv[s, k]
            total[s, lo + me, :, at] = part
            ref = total.at[s, lo + me, :, at]
            which = jnp.where(tile >= PARTS[0][1], 1, 0)
            for k in sorted(range(1, NZ), key=lambda d: -min(d, NZ - d)):
                to = device(x, y, lax.rem(z + k, NZ), core)
                remote(ref, ref, s_zg, r_zg.at[s, which], to).start()

        def to_core(p):
            ref = total.at[s, pl.ds(lo, XY), :, lanes(p)]
            return remote(ref, ref, s_cg.at[p], r_cg.at[s, p], partner)

        for p in range(N_PARTS):
            first, last = PARTS[p]
            mine_too = jnp.logical_and(owner, jnp.logical_and(tile >= first, tile < last))

            @pl.when(mine_too)
            def _():
                wait_bytes(mine.at[:, pl.ds(0, (last - first - 1) * 128)], r_zg.at[s, p])

            @pl.when(jnp.logical_not(mine_too))
            def _():
                wait_bytes(mine.at[:, pl.ds(0, (last - first) * 128)], r_zg.at[s, p])

            ref = total.at[s, lo + me, :, lanes(p)]
            for d, _ in plane:
                remote(ref, ref, s_xg.at[p], r_xg.at[s, p], d).start()

        if MOVE:
            @pl.when(jnp.logical_and(more, x_lo == 0))
            def _():
                odd_moves[1].wait_recv()
                even_moves[2].start()
        if COMPUTE:
            @pl.when(more)
            def _():
                prep_index(s + 1)

        wait_bytes(xrecv.at[s, :, :, lanes(0)], r_xg.at[s, 0])
        to_core(0).start()

        @pl.when(more)
        def _():
            if MOVE:
                for c in move_head:
                    c.wait()
            if COMPUTE:
                prep_head(s + 1)

        wait_bytes(xrecv.at[s, :, :, lanes(1)], r_xg.at[s, 1])
        to_core(1).start()

        @pl.when(more)
        def _():
            if MOVE:
                @pl.when(x_lo == 1)
                def _():
                    for c in odd_moves:
                        c.wait_send()

                @pl.when(x_lo == 0)
                def _():
                    for c in even_moves:
                        c.wait_send()

                even_moves[0].wait_recv()
                even_moves[1].wait_recv()
            if COMPUTE:
                prep_tail(s + 1)

        if COMPUTE:
            @pl.when(jnp.logical_not(more))
            def _():
                head[...] = heads[STEPS - 1, :W].T
                head_sum[...] = heads[STEPS - 1, W:W + 1]
                tail[...] = tails[STEPS - 1, :W].T
                tail_sum[...] = tails[STEPS - 1, W:W + 1]
                for c in stores[:4]:
                    c.start()

        for p in range(N_PARTS):
            to_other(p).wait_send()
            wait_bytes(xrecv.at[s, :, :, lanes(p)], s_x.at[p])
            wait_bytes(xrecv.at[s, :, :, lanes(p)], s_xg.at[p])

        @pl.when(owner)
        def _():
            wait_bytes(zrecv.at[s], s_zg)
            wait_bytes(mine.at[:, pl.ds(0, (TILES - 1) * 128)], s_z)

        @pl.when(jnp.logical_not(owner))
        def _():
            wait_bytes(mine, s_z)

        for p in range(N_PARTS):
            to_core(p).wait()
            if COMPUTE:
                for j in range(*PARTS[p]):
                    at = slice(j * 128, (j + 1) * 128)
                    grad = total[s, :, :, at].reshape(W, 128)
                    new = rsum[:, at] + jnp.mean(grad * grad, axis=0, keepdims=True)
                    rsum[:, at] = new
                    part = relT[:, at] - LEARN_RATE * grad * lax.rsqrt(new)
                    relT[:, at] = part
                    relhl[:W, at], relhl[W:, at] = split(part)

                @pl.when(more)
                def _():
                    gather_relations(p)

                @pl.when(jnp.logical_not(more))
                def _():
                    for j in range(*PARTS[p]):
                        count = min(128, RELS - j * 128)
                        rel[j * 128:j * 128 + count] = relT[:, j * 128:(j + 1) * 128].T[:count]
                    stores[5 + p].start()

        if COMPUTE:
            @pl.when(more)
            def _():
                terms()
        return carry

    lax.fori_loop(0, STEPS, step, 0)

    rel_sum[...] = rsum[:, :RELS].reshape(RELS)
    stores[4].start()
    if not COMPUTE:
        for k, c in enumerate(stores):
            if k != 4:
                c.start()
    for c in stores:
        c.wait()


PIECES = [(k, pl.ds(n, 256)) for k in (0, 2) for n in (0, 256)] + [(4, pl.ds(n, min(256, RELS - n))) for n in range(0, RELS, 256)]
PIECES += [(k, slice(None)) for k in (1, 3, 5)]


def write_out(*refs):
    ins, outs, kept, (s_read, s_write) = refs[:6], refs[6:12], refs[12:18], refs[18:]
    read, write = [], []
    for n, (k, rows) in enumerate(PIECES):
        src, mid, dst = ins[k], kept[k], outs[k]
        if not isinstance(rows, slice):
            src, mid, dst = src.at[rows], mid.at[rows], dst.at[rows]
        read.append(pltpu.make_async_copy(src, mid, s_read.at[n]))
        write.append(pltpu.make_async_copy(mid, dst, s_write.at[n]))
    for c in read:
        c.start()
    for c, d in zip(read, write):
        c.wait()
        d.start()
    for d in write:
        d.wait()


def held():
    shapes = ((ROWS, W), (1, ROWS), (ROWS, W), (1, ROWS), (RELS, W), (RELS,))
    return tuple(jax.ShapeDtypeStruct(shape, F32) for shape in shapes)


def window(head, head_state, tail, tail_state, relations, relation_state, edge_heads, edge_rels, edge_tails, negatives):
    dma, vmem = pltpu.SemaphoreType.DMA, pltpu.VMEM
    in_hbm = pl.BlockSpec(memory_space=pltpu.HBM)
    return pl.pallas_call(
        kernel,
        out_shape=held(),
        in_specs=[in_hbm] * 10,
        out_specs=[in_hbm] * 6,
        scratch_shapes=[
            vmem((ROWS, W), F32),
            vmem((ROWS, W), F32),
            vmem((RELS, W), F32),
            vmem((STEPS, 1, EDGES), jnp.int32),
            vmem((STEPS, 1, EDGES), jnp.int32),
            vmem((STEPS, 1, EDGES), jnp.int32),
            vmem((STEPS, BLOCKS, NEG), jnp.int32),
            vmem((1, ROWS), F32),
            vmem((1, ROWS), F32),
            vmem((RELS,), F32),
            dma((10,)),
            vmem((STEPS, SLAB, ROWS), F32),
            vmem((2 * STEPS, SLAB, ROWS), F32),
            vmem((W, RPAD), F32),
            vmem((1, RPAD), F32),
            vmem((2 * W, RPAD), BF16),
            vmem((RPAD, EDGES), BF16),
            vmem((ROWS, EDGES), BF16),
            vmem((ROWS, EDGES), BF16),
            vmem((ROWS, EDGES), F32),
            vmem((W, EDGES), F32),
            vmem((W, EDGES), F32),
            vmem((W, EDGES), F32),
            vmem((ROWS, W), BF16),
            vmem((W, ROWS), BF16),
            vmem((W, EDGES), F32),
            vmem((1, EDGES), F32),
            vmem((W, EDGES), BF16),
            vmem((ROWS, EDGES), BF16),
            vmem((ROWS, EDGES), BF16),
            vmem((W, EDGES), F32),
            vmem((2, W, EDGES), BF16),
            vmem((2 * XY, 8, RPAD), F32),
            vmem((STEPS, 2 * XY, 8, RPAD), F32),
            vmem((STEPS, XY, 8, RPAD), F32),
            vmem((XY, 8, RPAD), F32),
            vmem((STEPS, N_OFF, 8, RPAD), F32),
            vmem((STEPS, NZ - 1, 8, 128), F32),
            vmem((8, RPAD), F32),
            dma((N_PARTS,)), dma((STEPS, N_PARTS)),
            dma((N_PARTS,)), dma((STEPS, N_PARTS)),
            dma, dma((STEPS,)),
            dma, dma((STEPS, N_PARTS)),
            dma((N_PARTS,)), dma((STEPS, N_PARTS)),
            dma((N_PARTS,)), dma((STEPS, N_PARTS)),
            dma((2,)), dma((STEPS, 2)),
            dma((3,)), dma((STEPS, 2)), dma((STEPS,)),
        ],
        compiler_params=pltpu.CompilerParams(
            collective_id=0, has_side_effects=True, vmem_limit_bytes=VMEM_LIMIT
        ),
        name="window",
    )(
        head.reshape(ROWS, W),
        head_state.reshape(1, ROWS),
        tail.reshape(ROWS, W),
        tail_state.reshape(1, ROWS),
        relations,
        relation_state,
        edge_heads.reshape(STEPS, 1, EDGES),
        edge_rels.reshape(STEPS, 1, EDGES),
        edge_tails.reshape(STEPS, 1, EDGES),
        negatives.reshape(STEPS, BLOCKS, NEG),
    )


def body(*args):
    out = window(*args)
    dma, vmem = pltpu.SemaphoreType.DMA, pltpu.VMEM
    in_hbm = pl.BlockSpec(memory_space=pltpu.HBM)
    out = pl.pallas_call(
        write_out,
        out_shape=held(),
        in_specs=[in_hbm] * 6,
        out_specs=[in_hbm] * 6,
        scratch_shapes=[vmem(h.shape, F32) for h in held()] + [dma((len(PIECES),))] * 2,
        compiler_params=pltpu.CompilerParams(vmem_limit_bytes=VMEM_LIMIT),
        name="write_out",
    )(*out)
    return (
        out[0].reshape(1, 1, ROWS, W),
        out[1].reshape(1, 1, ROWS),
        out[2].reshape(1, 1, ROWS, W),
        out[3].reshape(1, 1, ROWS),
        out[4],
        out[5],
    )


def solution(mesh):
    slab, sums = P("lhs", "rhs", None, None), P("lhs", "rhs", None)
    return jax.shard_map(
        body,
        mesh=mesh,
        in_specs=(slab, sums, slab, sums, P(), P(), slab, slab, slab, P("lhs", "rhs", None, None, None)),
        out_specs=(slab, sums, slab, sums, P(), P()),
        check_vma=False,
    )
```

```python
import functools

import jax
import jax.numpy as jnp
from jax import lax
from jax.experimental import pallas as pl
from jax.experimental.pallas import tpu as pltpu
from jax.sharding import PartitionSpec as P

LEARN_RATE = 0.1
MESH = pl.DeviceIdType.MESH
F32, BF16 = jnp.float32, jnp.bfloat16

NX, NY, NZ = 4, 4, 16
N_LHS, N_RHS = 2 * NY * 2, NZ * 2
XY = NX * NY
W, HALF, ROWS, EDGES, RELS, STEPS = 256, 128, 512, 512, 1300, 3
BLOCKS, NEG = 4, 256
BLOCK = EDGES // BLOCKS
TILES = -(-RELS // 128)
RPAD = TILES * 128
SLAB = W + 8
HALVES = (pl.ds(0, 136), pl.ds(136, SLAB - 136))

PARTS = ((0, 6), (6, 11))
N_PARTS = len(PARTS)
OFFS = sorted(
    [(dx, dy) for dx in range(NX) for dy in range(NY) if (dx, dy) != (0, 0)],
    key=lambda o: -(min(o[0], NX - o[0]) + min(o[1], NY - o[1])),
)
N_OFF = len(OFFS)
OWN = [j * NZ // TILES for j in range(TILES)]
COMPUTE = True
MOVE = True
VMEM_LIMIT = 60 * 2**20


def coords():
    a, b = lax.axis_index("lhs"), lax.axis_index("rhs")
    core, y, xh = lax.rem(a, 2), lax.rem(lax.div(a, 2), NY), lax.div(a, 2 * NY)
    return xh * 2 + lax.rem(b, 2), y, lax.div(b, 2), core


def device(x, y, z, core):
    return ((lax.div(x, 2) * NY + y) * 2 + core, z * 2 + lax.rem(x, 2))


def nn(a, b):
    return jnp.dot(a, b, preferred_element_type=F32)


def nt(a, b):
    return lax.dot_general(a, b, (((1,), (1,)), ((), ())), preferred_element_type=F32)


def split(x):
    hi = x.astype(BF16)
    return hi, (x - hi.astype(F32)).astype(BF16)


def one_hot(index, count):
    place = lax.broadcasted_iota(jnp.int32, (count, index.shape[1]), 0)
    return jnp.where(place == index, 1.0, 0.0).astype(BF16)


def remote(src, dst, send, recv, to):
    return pltpu.make_async_remote_copy(
        src_ref=src, dst_ref=dst, send_sem=send, recv_sem=recv, device_id=to, device_id_type=MESH
    )


def wait_bytes(like, sem):
    pltpu.make_async_copy(like, like, sem).wait()


def kernel(
    head_in, head_sum_in, tail_in, tail_sum_in, rel_in, rel_sum_in, eh_in, er_in, et_in, ng_in,
    head_out, head_sum_out, tail_out, tail_sum_out, rel_out, rel_sum_out,
    head, tail, rel, eh, er, et, ng, head_sum, tail_sum, rel_sum, s_in,
    heads, tails, relT, rsum, relhl, oh_r, oh_h, oh_t, cnt,
    hT, tT, rT, tb, tbT, q, dpos, qb, phi, plo, gq, grhl,
    g, total, crecv, acc, xrecv, zrecv, mine,
    s_c, r_c, s_x, r_x, s_z, r_z, s_zg, r_zg, s_xg, r_xg, s_cg, r_cg, s_h, r_h, s_t, r_t, r_tb,
):
    x, y, z, core = coords()
    me = x * NY + y
    lo, other = core * XY, (1 - core) * XY
    a, b = lax.axis_index("lhs"), lax.axis_index("rhs")
    partner = device(x, y, z, 1 - core)
    head_to, head_from = (lax.rem(a + 1, N_LHS), b), (lax.rem(a + N_LHS - 1, N_LHS), b)
    plane = []
    sign = 1 - 2 * lax.rem(x + y, 2)
    for dx, dy in OFFS:
        ex, ey = dx + core * (dy - dx), dy + core * (dx - dy)
        tx, ty = lax.rem(x + sign * ex + NX, NX), lax.rem(y + sign * ey + NY, NY)
        plane.append((device(tx, ty, z, core), tx * NY + ty))

    barrier = pltpu.get_barrier_semaphore()
    peers = [device(x, y, lax.rem(z + dz, NZ), core) for dz in range(1, NZ)]
    peers += [d for d, _ in plane] + [partner, head_to, head_from]
    for d in peers:
        pl.semaphore_signal(barrier, inc=1, device_id=d, device_id_type=MESH)

    loads = [
        (er_in, er), (eh_in, eh), (et_in, et), (ng_in, ng), (head_in, head), (tail_in, tail), (rel_in, rel),
        (head_sum_in, head_sum), (tail_sum_in, tail_sum), (rel_sum_in, rel_sum),
    ]
    loads = [pltpu.make_async_copy(src, dst, s_in.at[k]) for k, (src, dst) in enumerate(loads)]
    for c in loads:
        c.start()

    stores = [
        (head, head_out), (head_sum, head_sum_out), (tail, tail_out), (tail_sum, tail_sum_out),
        (rel_sum, rel_sum_out),
    ]
    for first, last in PARTS:
        rows = pl.ds(first * 128, min(last * 128, RELS) - first * 128)
        stores.append((rel.at[rows], rel_out.at[rows]))
    stores = [pltpu.make_async_copy(src, dst, s_in.at[k]) for k, (src, dst) in enumerate(stores)]

    def prep_index(s):
        oh_r[...] = one_hot(er[s], RPAD)
        oh_h[...] = one_hot(eh[s], ROWS)
        oh_t[...] = one_hot(et[s], ROWS)
        ones = jnp.ones((NEG, BLOCK), BF16)
        for k in range(BLOCKS):
            cnt[:, k * BLOCK:(k + 1) * BLOCK] = nn(one_hot(ng[s, k:k + 1], ROWS), ones)

    def gather(wide, hot):
        both = nn(jnp.concatenate(split(wide), axis=0), hot)
        return both[:W] + both[W:]

    def prep_head(s):
        hT[...] = gather(heads[s, :W], oh_h[...])

    def prep_tail(s):
        slab = tails[s, :W]
        tT[...] = gather(slab, oh_t[...])
        tbT[...] = slab.astype(BF16)
        tb[...] = slab.T.astype(BF16)

    def update(slab, total_grad):
        new = slab[W:W + 1] + jnp.mean(total_grad * total_grad, axis=0, keepdims=True)
        slab[W:W + 1] = new
        slab[:W] = slab[:W] - LEARN_RATE * total_grad * lax.rsqrt(new)

    def lanes(p):
        return pl.ds(PARTS[p][0] * 128, (PARTS[p][1] - PARTS[p][0]) * 128)

    def relation_grad(k, p):
        both = nt(grhl[k], oh_r[lanes(p)])
        g[pl.ds(k * XY, XY), :, lanes(p)] = (both[:HALF] + both[HALF:]).reshape(XY, 8, -1)

    def gather_relations(p):
        both = nn(relhl[:, lanes(p)], oh_r[lanes(p)])
        part = both[:W] + both[W:]
        rT[...] = part if p == 0 else rT[...] + part

    def terms():
        r_re, r_im = rT[:HALF], rT[HALF:]
        h_re, h_im = hT[:HALF], hT[HALF:]
        q_re, q_im = h_re * r_re - h_im * r_im, h_re * r_im + h_im * r_re
        q[:HALF], q[HALF:] = q_re, q_im
        pos = jnp.sum(q_re * tT[:HALF] + q_im * tT[HALF:], axis=0, keepdims=True)
        dp = -jax.nn.sigmoid(-pos)
        dpos[...] = dp
        qb[:HALF], qb[HALF:] = q_re.astype(BF16), q_im.astype(BF16)
        scores = nn(tb[...], qb[...])
        dneg = (jax.nn.sigmoid(scores) * (1.0 / NEG)).astype(BF16)
        phi[...], plo[...] = split(dneg.astype(F32) * cnt[...])
        grad_q = dp * tT[...] + (nn(tbT[...], phi[...]) + nn(tbT[...], plo[...]))
        gq[...] = grad_q
        g_re, g_im = grad_q[:HALF], grad_q[HALF:]
        for k, term in enumerate((g_re * h_re + g_im * h_im, g_im * h_re - g_re * h_im)):
            grhl[k, :HALF], grhl[k, HALF:] = split(term)
        relation_grad(1 - core, 0)

    def head_update(s):
        g_re, g_im = gq[:HALF], gq[HALF:]
        r_re, r_im = rT[:HALF], rT[HALF:]
        term = jnp.concatenate([g_re * r_re + g_im * r_im, g_im * r_re - g_re * r_im], axis=0)
        both = nt(jnp.concatenate(split(term), axis=0), oh_h[...])
        update(heads.at[s], both[:W] + both[W:])

    def tail_update(s):
        term = dpos[...] * q[...]
        both = nt(jnp.concatenate(split(term), axis=0), oh_t[...])
        neg = nt(qb[...], phi[...]) + nt(qb[...], plo[...])
        update(tails.at[s], both[:W] + both[W:] + neg)

    if COMPUTE:
        for c in loads[:4]:
            c.wait()
        prep_index(0)
        for c in loads[4:]:
            c.wait()
        rsum[...] = jnp.ones_like(rsum)
        rsum[:, :RELS] = rel_sum[...].reshape(1, RELS)
        heads[0, :W] = head[...].T
        heads[0, W:W + 1] = head_sum[...]
        prep_head(0)
        tails[0, :W] = tail[...].T
        tails[0, W:W + 1] = tail_sum[...]
        prep_tail(0)
        for j in range(TILES):
            at = slice(j * 128, (j + 1) * 128)
            count = min(128, RELS - j * 128)
            part = rel[j * 128:j * 128 + count]
            if count < 128:
                part = jnp.concatenate([part, jnp.zeros((128 - count, W), F32)], axis=0)
            part = part.T
            relT[:, at] = part
            relhl[:W, at], relhl[W:, at] = split(part)
        for p in range(N_PARTS):
            gather_relations(p)
        terms()
    else:
        for c in loads:
            c.wait()
    pl.semaphore_wait(barrier, len(peers))

    x_lo = lax.rem(b, 2)
    tile = z - lax.div(z, 3)
    owner = jnp.logical_or(z == 0, lax.rem(z, 3) != 0)

    def step(s, carry):
        more = s < STEPS - 1
        move_head = [
            remote(heads.at[s, rows], heads.at[s + 1, rows], s_h.at[k], r_h.at[s, k], head_to)
            for k, rows in enumerate(HALVES)
        ]
        along_z = (a, lax.rem(b + 2, N_RHS))
        along_x = (a, b + 1 - 2 * x_lo)
        first, second = HALVES
        here, there, between = tails.at[s], tails.at[s + 1], tails.at[STEPS + s]
        odd_moves = (
            remote(here.at[first], between.at[first], s_t.at[0], r_tb.at[s], along_z),
            remote(here.at[second], between.at[second], s_t.at[1], r_tb.at[s], along_x),
            remote(between.at[first], there.at[first], s_t.at[2], r_t.at[s, 0], along_x),
        )
        even_moves = (
            remote(here.at[first], there.at[first], s_t.at[0], r_t.at[s, 0], along_x),
            remote(here.at[second], there.at[second], s_t.at[1], r_t.at[s, 1], along_x),
            remote(between.at[second], there.at[second], s_t.at[2], r_t.at[s, 1], along_z),
        )

        def to_other(p):
            return remote(
                g.at[pl.ds(other, XY), :, lanes(p)], crecv.at[s, :, :, lanes(p)], s_c.at[p], r_c.at[s, p], partner
            )

        def to_plane(p):
            to_other(p).wait_recv()
            for k, (d, t) in enumerate(plane):
                acc[t, :, lanes(p)] = g[lo + t, :, lanes(p)] + crecv[s, t, :, lanes(p)]
                remote(acc.at[t, :, lanes(p)], xrecv.at[s, k, :, lanes(p)], s_x.at[p], r_x.at[s, p], d).start()
            mine[:, lanes(p)] = g[lo + me, :, lanes(p)] + crecv[s, me, :, lanes(p)]

        to_other(0).start()
        if COMPUTE:
            relation_grad(1 - core, 1)
        to_other(1).start()
        if COMPUTE:
            relation_grad(core, 0)
        to_plane(0)
        if COMPUTE:
            relation_grad(core, 1)
        to_plane(1)

        if COMPUTE:
            tail_update(s)
        if MOVE:
            @pl.when(jnp.logical_and(more, x_lo == 1))
            def _():
                odd_moves[0].start()
        if COMPUTE:
            head_update(s)
        if MOVE:
            @pl.when(more)
            def _():
                for c in move_head:
                    c.start()


        for p in range(N_PARTS):
            wait_bytes(xrecv.at[s, :, :, lanes(p)], r_x.at[s, p])
            part = mine[:, lanes(p)]
            for k in range(N_OFF):
                part = part + xrecv[s, k, :, lanes(p)]
            mine[:, lanes(p)] = part
            for j in range(*PARTS[p]):
                @pl.when(z != OWN[j])
                def _():
                    remote(
                        mine.at[:, pl.ds(j * 128, 128)], zrecv.at[s, lax.rem(z - OWN[j] + NZ, NZ) - 1],
                        s_z, r_z.at[s], device(x, y, OWN[j], core),
                    ).start()

        if MOVE:
            @pl.when(more)
            def _():
                @pl.when(x_lo == 1)
                def _():
                    odd_moves[1].start()
                    odd_moves[0].wait_recv()
                    odd_moves[2].start()

                @pl.when(x_lo == 0)
                def _():
                    even_moves[0].start()
                    even_moves[1].start()

        @pl.when(owner)
        def _():
            wait_bytes(zrecv.at[s], r_z.at[s])
            at = pl.ds(pl.multiple_of(tile * 128, 128), 128)
            part = mine[:, at]
            for k in range(NZ - 1):
                part = part + zrecv[s, k]
            total[s, lo + me, :, at] = part
            ref = total.at[s, lo + me, :, at]
            which = jnp.where(tile >= PARTS[0][1], 1, 0)
            for k in sorted(range(1, NZ), key=lambda d: -min(d, NZ - d)):
                to = device(x, y, lax.rem(z + k, NZ), core)
                remote(ref, ref, s_zg, r_zg.at[s, which], to).start()

        def to_core(p):
            ref = total.at[s, pl.ds(lo, XY), :, lanes(p)]
            return remote(ref, ref, s_cg.at[p], r_cg.at[s, p], partner)

        for p in range(N_PARTS):
            first, last = PARTS[p]
            mine_too = jnp.logical_and(owner, jnp.logical_and(tile >= first, tile < last))

            @pl.when(mine_too)
            def _():
                wait_bytes(mine.at[:, pl.ds(0, (last - first - 1) * 128)], r_zg.at[s, p])

            @pl.when(jnp.logical_not(mine_too))
            def _():
                wait_bytes(mine.at[:, pl.ds(0, (last - first) * 128)], r_zg.at[s, p])

            ref = total.at[s, lo + me, :, lanes(p)]
            for d, _ in plane:
                remote(ref, ref, s_xg.at[p], r_xg.at[s, p], d).start()

        if MOVE:
            @pl.when(jnp.logical_and(more, x_lo == 0))
            def _():
                odd_moves[1].wait_recv()
                even_moves[2].start()
        if COMPUTE:
            @pl.when(more)
            def _():
                prep_index(s + 1)

        wait_bytes(xrecv.at[s, :, :, lanes(0)], r_xg.at[s, 0])
        to_core(0).start()

        @pl.when(more)
        def _():
            if MOVE:
                for c in move_head:
                    c.wait()
            if COMPUTE:
                prep_head(s + 1)

        wait_bytes(xrecv.at[s, :, :, lanes(1)], r_xg.at[s, 1])
        to_core(1).start()

        @pl.when(more)
        def _():
            if MOVE:
                @pl.when(x_lo == 1)
                def _():
                    for c in odd_moves:
                        c.wait_send()

                @pl.when(x_lo == 0)
                def _():
                    for c in even_moves:
                        c.wait_send()

                even_moves[0].wait_recv()
                even_moves[1].wait_recv()
            if COMPUTE:
                prep_tail(s + 1)

        if COMPUTE:
            @pl.when(jnp.logical_not(more))
            def _():
                head[...] = heads[STEPS - 1, :W].T
                head_sum[...] = heads[STEPS - 1, W:W + 1]
                tail[...] = tails[STEPS - 1, :W].T
                tail_sum[...] = tails[STEPS - 1, W:W + 1]
                for c in stores[:4]:
                    c.start()

        for p in range(N_PARTS):
            to_other(p).wait_send()
            wait_bytes(xrecv.at[s, :, :, lanes(p)], s_x.at[p])
            wait_bytes(xrecv.at[s, :, :, lanes(p)], s_xg.at[p])

        @pl.when(owner)
        def _():
            wait_bytes(zrecv.at[s], s_zg)
            wait_bytes(mine.at[:, pl.ds(0, (TILES - 1) * 128)], s_z)

        @pl.when(jnp.logical_not(owner))
        def _():
            wait_bytes(mine, s_z)

        for p in range(N_PARTS):
            to_core(p).wait()
            if COMPUTE:
                for j in range(*PARTS[p]):
                    at = slice(j * 128, (j + 1) * 128)
                    grad = total[s, :, :, at].reshape(W, 128)
                    new = rsum[:, at] + jnp.mean(grad * grad, axis=0, keepdims=True)
                    rsum[:, at] = new
                    part = relT[:, at] - LEARN_RATE * grad * lax.rsqrt(new)
                    relT[:, at] = part
                    relhl[:W, at], relhl[W:, at] = split(part)

                @pl.when(more)
                def _():
                    gather_relations(p)

                @pl.when(jnp.logical_not(more))
                def _():
                    for j in range(*PARTS[p]):
                        count = min(128, RELS - j * 128)
                        rel[j * 128:j * 128 + count] = relT[:, j * 128:(j + 1) * 128].T[:count]
                    stores[5 + p].start()

        if COMPUTE:
            @pl.when(more)
            def _():
                terms()
        return carry

    lax.fori_loop(0, STEPS, step, 0)

    rel_sum[...] = rsum[:, :RELS].reshape(RELS)
    stores[4].start()
    if not COMPUTE:
        for k, c in enumerate(stores):
            if k != 4:
                c.start()
    for c in stores:
        c.wait()


PIECES = [(k, pl.ds(n, 256)) for k in (0, 2) for n in (0, 256)] + [(4, pl.ds(n, min(256, RELS - n))) for n in range(0, RELS, 256)]
PIECES += [(k, slice(None)) for k in (1, 3, 5)]


def write_out(*refs):
    ins, outs, kept, (s_read, s_write) = refs[:6], refs[6:12], refs[12:18], refs[18:]
    read, write = [], []
    for n, (k, rows) in enumerate(PIECES):
        src, mid, dst = ins[k], kept[k], outs[k]
        if not isinstance(rows, slice):
            src, mid, dst = src.at[rows], mid.at[rows], dst.at[rows]
        read.append(pltpu.make_async_copy(src, mid, s_read.at[n]))
        write.append(pltpu.make_async_copy(mid, dst, s_write.at[n]))
    for c in read:
        c.start()
    for c, d in zip(read, write):
        c.wait()
        d.start()
    for d in write:
        d.wait()


def held():
    shapes = ((ROWS, W), (1, ROWS), (ROWS, W), (1, ROWS), (RELS, W), (RELS,))
    return tuple(jax.ShapeDtypeStruct(shape, F32) for shape in shapes)


def window(head, head_state, tail, tail_state, relations, relation_state, edge_heads, edge_rels, edge_tails, negatives):
    dma, vmem = pltpu.SemaphoreType.DMA, pltpu.VMEM
    in_hbm = pl.BlockSpec(memory_space=pltpu.HBM)
    return pl.pallas_call(
        kernel,
        out_shape=held(),
        in_specs=[in_hbm] * 10,
        out_specs=[in_hbm] * 6,
        scratch_shapes=[
            vmem((ROWS, W), F32),
            vmem((ROWS, W), F32),
            vmem((RELS, W), F32),
            vmem((STEPS, 1, EDGES), jnp.int32),
            vmem((STEPS, 1, EDGES), jnp.int32),
            vmem((STEPS, 1, EDGES), jnp.int32),
            vmem((STEPS, BLOCKS, NEG), jnp.int32),
            vmem((1, ROWS), F32),
            vmem((1, ROWS), F32),
            vmem((RELS,), F32),
            dma((10,)),
            vmem((STEPS, SLAB, ROWS), F32),
            vmem((2 * STEPS, SLAB, ROWS), F32),
            vmem((W, RPAD), F32),
            vmem((1, RPAD), F32),
            vmem((2 * W, RPAD), BF16),
            vmem((RPAD, EDGES), BF16),
            vmem((ROWS, EDGES), BF16),
            vmem((ROWS, EDGES), BF16),
            vmem((ROWS, EDGES), F32),
            vmem((W, EDGES), F32),
            vmem((W, EDGES), F32),
            vmem((W, EDGES), F32),
            vmem((ROWS, W), BF16),
            vmem((W, ROWS), BF16),
            vmem((W, EDGES), F32),
            vmem((1, EDGES), F32),
            vmem((W, EDGES), BF16),
            vmem((ROWS, EDGES), BF16),
            vmem((ROWS, EDGES), BF16),
            vmem((W, EDGES), F32),
            vmem((2, W, EDGES), BF16),
            vmem((2 * XY, 8, RPAD), F32),
            vmem((STEPS, 2 * XY, 8, RPAD), F32),
            vmem((STEPS, XY, 8, RPAD), F32),
            vmem((XY, 8, RPAD), F32),
            vmem((STEPS, N_OFF, 8, RPAD), F32),
            vmem((STEPS, NZ - 1, 8, 128), F32),
            vmem((8, RPAD), F32),
            dma((N_PARTS,)), dma((STEPS, N_PARTS)),
            dma((N_PARTS,)), dma((STEPS, N_PARTS)),
            dma, dma((STEPS,)),
            dma, dma((STEPS, N_PARTS)),
            dma((N_PARTS,)), dma((STEPS, N_PARTS)),
            dma((N_PARTS,)), dma((STEPS, N_PARTS)),
            dma((2,)), dma((STEPS, 2)),
            dma((3,)), dma((STEPS, 2)), dma((STEPS,)),
        ],
        compiler_params=pltpu.CompilerParams(
            collective_id=0, has_side_effects=True, vmem_limit_bytes=VMEM_LIMIT
        ),
        name="window",
    )(
        head.reshape(ROWS, W),
        head_state.reshape(1, ROWS),
        tail.reshape(ROWS, W),
        tail_state.reshape(1, ROWS),
        relations,
        relation_state,
        edge_heads.reshape(STEPS, 1, EDGES),
        edge_rels.reshape(STEPS, 1, EDGES),
        edge_tails.reshape(STEPS, 1, EDGES),
        negatives.reshape(STEPS, BLOCKS, NEG),
    )


def body(*args):
    out = window(*args)
    dma, vmem = pltpu.SemaphoreType.DMA, pltpu.VMEM
    in_hbm = pl.BlockSpec(memory_space=pltpu.HBM)
    out = pl.pallas_call(
        write_out,
        out_shape=held(),
        in_specs=[in_hbm] * 6,
        out_specs=[in_hbm] * 6,
        scratch_shapes=[vmem(h.shape, F32) for h in held()] + [dma((len(PIECES),))] * 2,
        compiler_params=pltpu.CompilerParams(vmem_limit_bytes=VMEM_LIMIT),
        name="write_out",
    )(*out)
    return (
        out[0].reshape(1, 1, ROWS, W),
        out[1].reshape(1, 1, ROWS),
        out[2].reshape(1, 1, ROWS, W),
        out[3].reshape(1, 1, ROWS),
        out[4],
        out[5],
    )


def solution(mesh):
    slab, sums = P("lhs", "rhs", None, None), P("lhs", "rhs", None)
    return jax.shard_map(
        body,
        mesh=mesh,
        in_specs=(slab, sums, slab, sums, P(), P(), slab, slab, slab, P("lhs", "rhs", None, None, None)),
        out_specs=(slab, sums, slab, sums, P(), P()),
        check_vma=False,
    )
```
